32 devices in a mesh: seq: 8 (over y, x, core), head: 4 (over z).
Axes of the slice: x: 2, y: 2, z: 4, core: 2. Of those that a mesh axis runs over, the one named last changes fastest.
Arguments:
- queries: bfloat16 [2048, 3072], P('seq', 'head'), may hold values from -6 to 6
- keys: bfloat16 [2048, 3072], P('seq', 'head'), may hold values from -6 to 6
- values: bfloat16 [2048, 3072], P('seq', 'head'), may hold values from -6 to 6
- grad_out: bfloat16 [2048, 3072], P('seq', 'head'), may hold values from -6 to 6
- scene_keys: bfloat16 [32, 3072], P(('seq', 'head')), may hold values from -6 to 6
- scene_values: bfloat16 [32, 3072], P(('seq', 'head')), may hold values from -6 to 6
- valid: int32 [32], replicated, may hold values from 2 to 64
- pattern: int32 [32, 3], replicated, may hold values from 0 to 31, as said below
Outputs:
- attended: bfloat16 [2048, 3072], P('seq', 'head')
- grad_queries: bfloat16 [2048, 3072], P('seq', 'head')
- grad_keys: bfloat16 [2048, 3072], P('seq', 'head')
- grad_values: bfloat16 [2048, 3072], P('seq', 'head')
- grad_scene_keys: bfloat16 [32, 3072], P(('seq', 'head'))
- grad_scene_values: bfloat16 [32, 3072], P(('seq', 'head'))
The draws below stay inside these ranges and needn't reach their ends.
Inputs may be any that keep to these rules, and one draw needn't show every extreme that they name: `pattern`: the 12 entries of the query blocks of one seq index all name blocks of other seq indices; no seq index supplies more than 2 of them to one seq index, and to each seq index some seq index supplies exactly 2.
All inputs are finite; a program needn't handle non-finite values.
Results may differ from the reference program's by a relative error of at most 0.0061.
Values may be sent and summed in bfloat16 or wider, within the bound.
A program may use at most 128 MiB of HBM per device.

```python
import jax
import jax.numpy as jnp
from jax import lax

HEADS = 24
DH = 128
BLK = 64
RAND = 3
BLK_DEV = 4
FEAT = 3072
NBLK = 32
TOKENS = 2048
SCENE = 32
N_HEAD = 4


def draw_queries(key, part):
    sample_key = jax.random.fold_in(key, 11)
    sample = jnp.clip(jax.random.normal(sample_key, (NBLK, BLK, FEAT), jnp.float32), -6.0, 6.0)
    return sample.reshape(TOKENS, FEAT).astype(jnp.bfloat16)


def draw_keys(key, part):
    sample_key = jax.random.fold_in(key, 12)
    sample = jnp.clip(jax.random.normal(sample_key, (NBLK, BLK, FEAT), jnp.float32), -6.0, 6.0)
    return sample.reshape(TOKENS, FEAT).astype(jnp.bfloat16)


def draw_pattern(key, part):
    seq_count = NBLK // BLK_DEV
    requests = BLK_DEV * RAND
    keys_first = jax.random.split(jax.random.fold_in(key, 5), seq_count)
    keys_second = jax.random.split(jax.random.fold_in(key, 6), seq_count)
    perms = jax.vmap(lambda subkey: jax.random.permutation(subkey, seq_count - 1))(keys_first)
    orders = jax.vmap(lambda subkey: jax.random.permutation(subkey, requests))(keys_second)
    column = jnp.arange(requests, dtype=jnp.int32) % (seq_count - 1)
    offset = perms[:, column] + 1
    offset = jnp.take_along_axis(offset, orders, axis=1)
    device = (jnp.arange(seq_count, dtype=jnp.int32)[:, None] + offset) % seq_count
    block = jax.random.randint(jax.random.fold_in(key, 7), (seq_count, requests), 0, BLK_DEV)
    return (device * BLK_DEV + block).reshape(NBLK, RAND).astype(jnp.int32)


def with_ends(entries, own_key, least, top_value):
    longest = entries.shape.index(max(entries.shape))
    spots = []
    for shift in (0, 1):
        where = [jax.random.randint(jax.random.fold_in(own_key, axis), (), 0, length) for axis, length in enumerate(entries.shape)]
        where[longest] = (where[longest] + shift) % entries.shape[longest]
        spots.append(tuple(where))
    return entries.at[spots[0]].set(least).at[spots[1]].set(top_value)


def shard_levels(stream_key, dims, pieces, least, largest):
    def one(position, parts):
        draws = jax.random.uniform(jax.random.fold_in(jax.random.fold_in(stream_key, 6), position), (parts,), jnp.float32, least / len(pieces), largest / len(pieces))
        return jnp.repeat(jnp.exp(draws), dims[position] // parts).reshape((-1,) + (1,) * (len(dims) - position - 1))

    loudness = one(*pieces[0])
    for cut in pieces[1:]:
        loudness = loudness * one(*cut)
    return loudness


def normal_values(stream_key, extent, scale, reach, shards=(), kind=jnp.bfloat16):
    values = scale * jax.random.normal(stream_key, extent, jnp.float32)
    if shards:
        values = values * shard_levels(stream_key, extent, shards, -0.22, 0.18)
    return jnp.clip(values, -reach, reach).astype(kind)


def setup_inputs(seed: int = 0) -> dict:
    key_list = jax.random.split(jax.random.key(seed), 9)
    return {
        "queries": draw_queries(jax.random.fold_in(key_list[8], 71), 0),
        "keys": draw_keys(jax.random.fold_in(key_list[8], 71), 0),
        "values": normal_values(key_list[2], (TOKENS, FEAT), 1.0, 6.0, ((0, 8), (1, 4))),
        "grad_out": normal_values(key_list[3], (TOKENS, FEAT), 1.0, 6.0, ((0, 8), (1, 4))),
        "scene_keys": normal_values(key_list[4], (SCENE, FEAT), 1.0, 6.0, ((0, 32),)),
        "scene_values": normal_values(key_list[5], (SCENE, FEAT), 1.0, 6.0, ((0, 32),)),
        "valid": with_ends(jax.random.randint(key_list[6], (NBLK,), 2, BLK + 1), jax.random.fold_in(key_list[6], 1), 2, BLK).astype(jnp.int32),
        "pattern": draw_pattern(jax.random.fold_in(key_list[8], 71), 0),
    }


def rounded(value):
    return lax.optimization_barrier(value.astype(jnp.bfloat16)).astype(jnp.float32)


def block_terms(query, near_keys, near_values, scene_k, scene_v, key_live, query_live, grad_out):
    scale = DH ** -0.5
    near_scores = jnp.einsum('gqhd,gkhd->ghqk', query, near_keys) * scale
    near_scores = jnp.where(key_live[:, None, None, :], near_scores, -1e30)
    scene_scores = jnp.einsum('gqhd,khd->ghqk', query, scene_k) * scale
    highest = jnp.maximum(jnp.max(near_scores, axis=3, keepdims=True), jnp.max(scene_scores, axis=3, keepdims=True))
    near_exp = jnp.exp(near_scores - highest)
    scene_exp = jnp.exp(scene_scores - highest)
    denominator = jnp.sum(near_exp, axis=3, keepdims=True) + jnp.sum(scene_exp, axis=3, keepdims=True)
    near_prob = near_exp / denominator
    scene_prob = scene_exp / denominator
    near_round = rounded(near_prob)
    scene_round = rounded(scene_prob)
    live_rows = query_live[:, :, None, None]
    attended = jnp.einsum('ghqk,gkhd->gqhd', near_round, near_values) + jnp.einsum('ghqk,khd->gqhd', scene_round, scene_v)
    attended = jnp.where(live_rows, attended, 0.0).astype(jnp.bfloat16)
    grad_live = jnp.where(live_rows, grad_out, 0.0)
    near_dprob = jnp.einsum('gqhd,gkhd->ghqk', grad_live, near_values)
    scene_dprob = jnp.einsum('gqhd,khd->ghqk', grad_live, scene_v)
    delta = jnp.sum(near_prob * near_dprob, axis=3, keepdims=True) + jnp.sum(scene_prob * scene_dprob, axis=3, keepdims=True)
    near_dscore = rounded(near_prob * (near_dprob - delta) * scale)
    scene_dscore = rounded(scene_prob * (scene_dprob - delta) * scale)
    grad_query = jnp.einsum('ghqk,gkhd->gqhd', near_dscore, near_keys) + jnp.einsum('ghqk,khd->gqhd', scene_dscore, scene_k)
    grad_near_k = jnp.einsum('ghqk,gqhd->gkhd', near_dscore, query)
    grad_near_v = jnp.einsum('ghqk,gqhd->gkhd', near_round, grad_live)
    grad_scene_k = jnp.einsum('ghqk,gqhd->khd', scene_dscore, query)
    grad_scene_v = jnp.einsum('ghqk,gqhd->khd', scene_round, grad_live)
    return attended, grad_query.astype(jnp.bfloat16), grad_near_k, grad_near_v, grad_scene_k, grad_scene_v


def add_near(total, terms, first_block, group_size):
    window_acc = lax.dynamic_slice_in_dim(total, first_block, group_size + 2, 0)
    window_acc = window_acc.at[0:group_size].add(terms[:, 0])
    window_acc = window_acc.at[1:group_size + 1].add(terms[:, 1])
    window_acc = window_acc.at[2:].add(terms[:, 2])
    return lax.dynamic_update_slice_in_dim(total, window_acc, first_block, 0)


def reference(queries, keys, values, grad_out, scene_keys, scene_values, valid, pattern):
    head_count = HEADS // N_HEAD
    features = head_count * DH
    group_size = min(8, BLK_DEV)
    offsets = jnp.arange(BLK, dtype=jnp.int32)
    padded_valid = jnp.concatenate([jnp.zeros((1,), jnp.int32), valid.astype(jnp.int32), jnp.zeros((1,), jnp.int32)])
    attended_list, gquery_list, gkey_list, gvalue_list, gscene_k_list, gscene_v_list = [], [], [], [], [], []
    for part_index in range(N_HEAD):
        column_low = part_index * features

        def columns(array):
            return array[:, column_low:column_low + features].astype(jnp.float32)

        query_all = columns(queries).reshape(NBLK, BLK, head_count, DH)
        key_all = columns(keys).reshape(NBLK, BLK, head_count, DH)
        value_all = columns(values).reshape(NBLK, BLK, head_count, DH)
        grad_all = columns(grad_out).reshape(NBLK, BLK, head_count, DH)
        key_pad = jnp.pad(key_all, ((1, 1), (0, 0), (0, 0), (0, 0)))
        value_pad = jnp.pad(value_all, ((1, 1), (0, 0), (0, 0), (0, 0)))
        scene_k = columns(scene_keys).reshape(SCENE, head_count, DH)
        scene_v = columns(scene_values).reshape(SCENE, head_count, DH)

        def advance(running, group_index):
            key_acc, value_acc, scene_k_acc, scene_v_acc = running
            first_block = group_index.astype(jnp.int32) * group_size
            query_grp = lax.dynamic_slice_in_dim(query_all, first_block, group_size, 0)
            grad_grp = lax.dynamic_slice_in_dim(grad_all, first_block, group_size, 0)
            window_k = lax.dynamic_slice_in_dim(key_pad, first_block, group_size + 2, 0)
            window_v = lax.dynamic_slice_in_dim(value_pad, first_block, group_size + 2, 0)
            random_ids = lax.dynamic_slice_in_dim(pattern, first_block, group_size, 0).astype(jnp.int32)
            near_k = jnp.concatenate([window_k[0:group_size, None], window_k[1:group_size + 1, None], window_k[2:, None], key_all[random_ids]], axis=1)
            near_v = jnp.concatenate([window_v[0:group_size, None], window_v[1:group_size + 1, None], window_v[2:, None], value_all[random_ids]], axis=1)
            near_k = near_k.reshape(group_size, (3 + RAND) * BLK, head_count, DH)
            near_v = near_v.reshape(group_size, (3 + RAND) * BLK, head_count, DH)
            window_count = lax.dynamic_slice_in_dim(padded_valid, first_block, group_size + 2, 0)
            counts = jnp.concatenate([window_count[0:group_size, None], window_count[1:group_size + 1, None], window_count[2:, None], valid[random_ids]], axis=1)
            key_live = (offsets[None, None, :] < counts[:, :, None]).reshape(group_size, (3 + RAND) * BLK)
            query_live = offsets[None, :] < lax.dynamic_slice_in_dim(valid, first_block, group_size, 0)[:, None]
            attended, grad_query, grad_k, grad_v, grad_sk, grad_sv = block_terms(query_grp, near_k, near_v, scene_k, scene_v, key_live, query_live, grad_grp)
            grad_k = grad_k.reshape(group_size, 3 + RAND, BLK, head_count, DH)
            grad_v = grad_v.reshape(group_size, 3 + RAND, BLK, head_count, DH)
            key_acc = add_near(key_acc, grad_k, first_block, group_size)
            value_acc = add_near(value_acc, grad_v, first_block, group_size)
            targets = random_ids.reshape(-1) + 1
            key_acc = key_acc.at[targets].add(rounded(grad_k[:, 3:]).reshape(group_size * RAND, BLK, head_count, DH))
            value_acc = value_acc.at[targets].add(rounded(grad_v[:, 3:]).reshape(group_size * RAND, BLK, head_count, DH))
            return (key_acc, value_acc, scene_k_acc + grad_sk, scene_v_acc + grad_sv), (attended, grad_query)

        initial = (jnp.zeros((NBLK + 2, BLK, head_count, DH), jnp.float32), jnp.zeros((NBLK + 2, BLK, head_count, DH), jnp.float32),
                   jnp.zeros((SCENE, head_count, DH), jnp.float32), jnp.zeros((SCENE, head_count, DH), jnp.float32))
        running, (attended_all, gquery_all) = lax.scan(advance, initial, jnp.arange(NBLK // group_size, dtype=jnp.int32))
        key_acc, value_acc, scene_k_acc, scene_v_acc = running
        attended_list.append(attended_all.reshape(TOKENS, features))
        gquery_list.append(gquery_all.reshape(TOKENS, features))
        gkey_list.append(key_acc[1:NBLK + 1].reshape(TOKENS, features).astype(jnp.bfloat16))
        gvalue_list.append(value_acc[1:NBLK + 1].reshape(TOKENS, features).astype(jnp.bfloat16))
        gscene_k_list.append(scene_k_acc.reshape(SCENE, features).astype(jnp.bfloat16))
        gscene_v_list.append(scene_v_acc.reshape(SCENE, features).astype(jnp.bfloat16))
    return (jnp.concatenate(attended_list, axis=1), jnp.concatenate(gquery_list, axis=1), jnp.concatenate(gkey_list, axis=1),
            jnp.concatenate(gvalue_list, axis=1), jnp.concatenate(gscene_k_list, axis=1), jnp.concatenate(gscene_v_list, axis=1))
```

```python
import functools

import jax
import jax.numpy as jnp
from jax import lax
from jax.experimental import pallas as pl
from jax.experimental.pallas import tpu as pltpu
from jax.sharding import PartitionSpec as P

DH = 128
BLK = 64
RAND = 3


def extended_2(block, sides, width):
    for axis, dim in sides:
        count = lax.axis_size(axis)
        forward = [(i, i + 1) for i in range(count - 1)]
        backward = [(target, source) for source, target in forward]
        low = lax.ppermute(
            lax.slice_in_dim(block, block.shape[dim] - width, None, axis=dim), axis, forward
        )
        high = lax.ppermute(lax.slice_in_dim(block, 0, width, axis=dim), axis, backward)
        block = jnp.concatenate([low, block, high], axis=dim)
    return block


def passed_along(x, axis, by):
    length = lax.axis_size(axis)
    pairs = [(i, i + by) for i in range(length) if 0 <= i + by < length]
    return lax.ppermute(x, axis, pairs)


def block_terms(query, all_keys, all_values, key_live, query_live, grad_out):
    scale = DH ** (-0.5)
    scores = (
        jnp.einsum("gqhd,gkhd->ghqk", query, all_keys, preferred_element_type=jnp.float32) * scale
    )
    scores = jnp.where(key_live[:, None, None, :], scores, -1e30)
    highest = jnp.max(scores, axis=3, keepdims=True)
    expo = jnp.exp(scores - highest)
    prob = expo / jnp.sum(expo, axis=3, keepdims=True)
    prob_round = prob.astype(jnp.bfloat16)
    live_rows = query_live[:, :, None, None]
    attended = jnp.einsum(
        "ghqk,gkhd->gqhd", prob_round, all_values, preferred_element_type=jnp.float32
    )
    attended = jnp.where(live_rows, attended, 0.0).astype(jnp.bfloat16)
    grad_live = jnp.where(live_rows, grad_out, 0.0)
    dprob = jnp.einsum("gqhd,gkhd->ghqk", grad_live, all_values, preferred_element_type=jnp.float32)
    delta = jnp.sum(prob * dprob, axis=3, keepdims=True)
    dscore = (prob * (dprob - delta) * scale).astype(jnp.bfloat16)
    grad_query = jnp.einsum("ghqk,gkhd->gqhd", dscore, all_keys, preferred_element_type=jnp.float32)
    grad_k = jnp.einsum("ghqk,gqhd->gkhd", dscore, query, preferred_element_type=jnp.float32)
    grad_v = jnp.einsum(
        "ghqk,gqhd->gkhd", prob_round, grad_live, preferred_element_type=jnp.float32
    )
    return (attended, grad_query.astype(jnp.bfloat16), grad_k, grad_v)


def per_device(queries, keys, values, grad_out, scene_keys, scene_values, valid, pattern):
    seq_count = lax.axis_size("seq")
    position = lax.axis_index("seq")
    features = queries.shape[1]
    head_count = features // DH
    blocks_dev = queries.shape[0] // BLK
    group_size = min(8, blocks_dev)
    requests = blocks_dev * RAND
    slot_count = (requests + seq_count - 2) // (seq_count - 1)
    offsets = jnp.arange(BLK, dtype=jnp.int32)
    near_count = (3 + RAND) * BLK
    parted = (
        lax.all_to_all(scene_keys, "head", split_axis=1, concat_axis=0, tiled=True),
        lax.all_to_all(scene_values, "head", split_axis=1, concat_axis=0, tiled=True),
    )
    scene_k, scene_v = (
        lax.all_gather(parted[0], "seq", axis=0, tiled=True),
        lax.all_gather(parted[1], "seq", axis=0, tiled=True),
    )
    scene_rows_all = scene_k.shape[0]
    scene_kv = jnp.stack([scene_k, scene_v]).reshape(2, 1, scene_rows_all, head_count, DH)
    scene_kv = jnp.broadcast_to(scene_kv, (2, group_size, scene_rows_all, head_count, DH))
    stacked = jnp.stack([keys, values])
    extended = extended_2(stacked, (("seq", 1),), BLK)
    all_requests = pattern.reshape(seq_count, requests)
    source = all_requests // blocks_dev
    local_block = all_requests % blocks_dev
    from_here = source == position
    send_rank = jnp.cumsum(from_here.astype(jnp.int32), axis=1) - 1
    slot_ids = jnp.arange(slot_count, dtype=jnp.int32)
    marked = from_here[:, :, None] & (send_rank[:, :, None] == slot_ids[None, None, :])
    chosen = jnp.sum(jnp.where(marked, local_block[:, :, None], 0), axis=1)
    block_view = stacked.reshape(2, blocks_dev, BLK, features)
    outgoing = block_view[:, chosen]
    incoming = lax.all_to_all(outgoing, "seq", split_axis=1, concat_axis=1, tiled=True)
    own_requests = lax.dynamic_slice_in_dim(pattern, position * blocks_dev, blocks_dev, 0).reshape(
        requests
    )
    own_source = own_requests // blocks_dev
    earlier = jnp.tril(jnp.ones((requests, requests), jnp.bool_), -1)
    same_source = own_source[:, None] == own_source[None, :]
    recv_rank = jnp.sum((same_source & earlier).astype(jnp.int32), axis=1)
    recv_place = own_source * slot_count + recv_rank
    far_blocks = incoming.reshape(2, seq_count * slot_count, BLK, features)[:, recv_place]
    far_blocks = far_blocks.reshape(2, blocks_dev, RAND, BLK, features)
    padded_valid = jnp.concatenate([jnp.zeros((1,), jnp.int32), valid, jnp.zeros((1,), jnp.int32)])
    window_count = lax.dynamic_slice_in_dim(padded_valid, position * blocks_dev, blocks_dev + 2, 0)
    far_count = valid[own_requests].reshape(blocks_dev, RAND)
    query_count = lax.dynamic_slice_in_dim(valid, position * blocks_dev, blocks_dev, 0)
    scene_live = jnp.ones((group_size, scene_rows_all), jnp.bool_)
    ext_grad = jnp.zeros((2, blocks_dev + 2, BLK, features), jnp.float32)
    query_grp = queries.reshape(group_size, BLK, head_count, DH)
    grad_grp = grad_out.reshape(group_size, BLK, head_count, DH)
    window = extended.reshape(2, group_size + 2, BLK, features)
    near_kv = jnp.concatenate(
        [
            window[:, 0:group_size, None],
            window[:, 1 : group_size + 1, None],
            window[:, 2:, None],
            far_blocks,
        ],
        axis=2,
    )
    near_kv = near_kv.reshape(2, group_size, near_count, head_count, DH)
    joined_kv = jnp.concatenate([near_kv, scene_kv], axis=2)
    counts = jnp.concatenate(
        [
            window_count[0:group_size, None],
            window_count[1 : group_size + 1, None],
            window_count[2 : group_size + 2, None],
            far_count,
        ],
        axis=1,
    )
    near_live = (offsets[None, None, :] < counts[:, :, None]).reshape(group_size, near_count)
    key_live = jnp.concatenate([near_live, scene_live], axis=1)
    query_live = offsets[None, :] < query_count[0:group_size, None]
    attended, grad_query, grad_k, grad_v = block_terms(
        query_grp, joined_kv[0], joined_kv[1], key_live, query_live, grad_grp
    )
    both_grad = jnp.stack([grad_k, grad_v])
    near_grad = both_grad[:, :, :near_count].reshape(2, group_size, 3 + RAND, BLK, features)
    scene_grad = jnp.sum(both_grad[:, :, near_count:], axis=1)
    ext_grad = ext_grad.at[:, 0:group_size].add(near_grad[:, :, 0])
    ext_grad = ext_grad.at[:, 1 : group_size + 1].add(near_grad[:, :, 1])
    ext_grad = ext_grad.at[:, 2 : group_size + 2].add(near_grad[:, :, 2])
    random_parts = near_grad[:, :, 3:].astype(jnp.bfloat16)
    attended_parts = attended.reshape(group_size * BLK, features)
    query_parts = grad_query.reshape(group_size * BLK, features)
    random_terms = random_parts.reshape(2, requests, BLK, features)
    outgoing_grad = (
        jnp.zeros((2, seq_count * slot_count, BLK, features), jnp.bfloat16)
        .at[:, recv_place]
        .set(random_terms)
    )
    outgoing_grad = outgoing_grad.reshape(2, seq_count, slot_count, BLK, features)
    returned = lax.all_to_all(outgoing_grad, "seq", split_axis=1, concat_axis=1, tiled=True)
    selector = (
        chosen.reshape(-1)[:, None] == jnp.arange(blocks_dev, dtype=jnp.int32)[None, :]
    ).astype(jnp.bfloat16)
    gathered_grad = jnp.einsum(
        "sb,xsk->xbk",
        selector,
        returned.reshape(2, seq_count * slot_count, BLK * features),
        preferred_element_type=jnp.float32,
    )
    from_right = passed_along(ext_grad[:, 0].astype(jnp.bfloat16), "seq", -1).astype(jnp.float32)
    from_left = passed_along(ext_grad[:, blocks_dev + 1].astype(jnp.bfloat16), "seq", 1).astype(
        jnp.float32
    )
    inner = ext_grad[:, 1 : blocks_dev + 1]
    inner = inner.at[:, blocks_dev - 1].add(from_right).at[:, 0].add(from_left)
    total_grad = inner.reshape(2, blocks_dev, BLK * features) + gathered_grad
    grad_keys = total_grad[0].reshape(blocks_dev * BLK, features).astype(jnp.bfloat16)
    grad_values = total_grad[1].reshape(blocks_dev * BLK, features).astype(jnp.bfloat16)
    scene_terms_k = scene_grad[0].reshape(scene_rows_all, features)
    scene_terms_v = scene_grad[1].reshape(scene_rows_all, features)
    mine_k, mine_v = (
        lax.psum_scatter(scene_terms_k, "seq", scatter_dimension=0, tiled=True),
        lax.psum_scatter(scene_terms_v, "seq", scatter_dimension=0, tiled=True),
    )
    back_k, back_v = (
        lax.all_to_all(mine_k, "head", split_axis=0, concat_axis=1, tiled=True),
        lax.all_to_all(mine_v, "head", split_axis=0, concat_axis=1, tiled=True),
    )
    return (
        attended_parts,
        query_parts,
        grad_keys,
        grad_values,
        back_k.astype(jnp.bfloat16),
        back_v.astype(jnp.bfloat16),
    )


NEG = -1e30
EXTRA = 16
MESH = pl.DeviceIdType.MESH
F32 = jnp.float32
BF16 = jnp.bfloat16


def fused_kernel(
    heads, n_head, blocks,
    valid_ref, pattern_ref, q_ref, k_ref, v_ref, g_ref, sc_ref,
    att_ref, gq_ref, gk_ref, gv_ref, sg_ref,
    kv, grads, rsib, rdiag, rdir, bias, sbuf, dbuf, pbuf, dsbuf, kt, vt, glive,
    sc_recv, sc_stage, sc_send,
    ag_send, ag_recv, rs_send, rs_recv, sc_ssem, sc_rsem, sg_ssem, sg_rsem,
):
    rows = blocks * BLK
    slot = rows + EXTRA
    total = 8 * slot
    p = lax.axis_index("seq")
    hd = lax.axis_index("head")
    nc = p + 1 - 2 * lax.rem(p, 2)
    nx = p + 2 - 4 * lax.rem(lax.div(p, 2), 2)
    ny = p + 4 - 8 * lax.rem(lax.div(p, 4), 2)
    nd = nx + ny - p
    flip = nc - p

    barrier = pltpu.get_barrier_semaphore()
    for target in (nc, nx, ny):
        pl.semaphore_signal(barrier, inc=1, device_id={"seq": target}, device_id_type=MESH)
    for d in range(1, n_head):
        pl.semaphore_signal(
            barrier, inc=1, device_id={"head": lax.rem(hd + d, n_head)}, device_id_type=MESH
        )
    pl.semaphore_wait(barrier, 3 + n_head - 1)

    def at_slot(ref, h, q):
        return ref.at[h, :, pl.ds(pl.multiple_of(q * slot, 16), slot), :]

    def at_half(ref, h, half, q):
        return ref.at[h, half, pl.ds(pl.multiple_of(q * slot, 16), slot), :]

    def copy(src, dst, ssem, rsem, dev):
        return pltpu.make_async_remote_copy(
            src_ref=src, dst_ref=dst, send_sem=ssem, recv_sem=rsem,
            device_id={"seq": dev}, device_id_type=MESH,
        )

    def ag(h, k, sending):
        sent, dev, arrives = (
            (p, nx, nx), (p, ny, ny), (p, nc, nc), (nx, ny, nd), (ny, nx, nd),
            (nx, nc, nx + flip), (ny, nc, ny + flip), (nd, nc, nd + flip),
        )[k]
        s = sent if sending else arrives
        ref = at_half(kv, h, k - 3, s) if k in (3, 4) else at_slot(kv, h, s)
        return copy(ref, ref, ag_send.at[h, k], ag_recv.at[h, k], dev)

    def rs(h, k):
        if k < 4:
            q = (p, nx, ny, nd)[k] + flip
            src, dst, dev = at_slot(grads, h, q), rsib.at[h, k], nc
        elif k < 6:
            src, dst = at_half(grads, h, k - 4, nd), rdiag.at[h, k - 4]
            dev = (nx, ny)[k - 4]
        else:
            dev = (nx, ny)[k - 6]
            src, dst = at_slot(grads, h, dev), rdir.at[h, k - 6]
        return copy(src, dst, rs_send.at[h, k], rs_recv.at[h, k], dev)

    def scene(d, src, dst, ssem, rsem):
        target = lax.rem(hd + d, n_head)
        return pltpu.make_async_remote_copy(
            src_ref=src.at[target], dst_ref=dst.at[hd], send_sem=ssem.at[d], recv_sem=rsem.at[d],
            device_id={"head": target}, device_id_type=MESH,
        )

    for d in range(1, n_head):
        scene(d, sc_ref, sc_recv, sc_ssem, sc_rsem).start()
    sc_recv[hd] = sc_ref[hd]
    own = pl.multiple_of(p * slot, 16)
    for h in range(heads):
        kv[h, 0, pl.ds(own, rows), :] = k_ref[:, h * DH:(h + 1) * DH]
        kv[h, 1, pl.ds(own, rows), :] = v_ref[:, h * DH:(h + 1) * DH]
    sc_stage[...] = jnp.zeros_like(sc_stage)
    for d in range(1, n_head):
        scene(d, sc_ref, sc_recv, sc_ssem, sc_rsem).wait()
    for h in range(heads):
        for half in range(2):
            for t in range(n_head):
                row = half * 8 + h
                sc_stage[h, half, t:t + 1, :] = sc_recv[t, row:row + 1, :]
            kv[h, half, pl.ds(pl.multiple_of(own + rows, 16), EXTRA), :] = sc_stage[
                h, half
            ].astype(BF16)
    for h in range(min(2, heads)):
        for k in range(3):
            ag(h, k, True).start()

    lane = lax.broadcasted_iota(jnp.int32, (1, rows), 1)
    lane_block = lax.div(lane, BLK)
    row_in = lax.broadcasted_iota(jnp.int32, (BLK, rows), 0)
    named = []
    for r in range(RAND):
        row = jnp.zeros((1, rows), jnp.int32)
        for b in range(blocks):
            row = jnp.where(lane_block == b, pattern_ref[p * blocks + b, r], row)
        named.append(row)
    query_block = lane_block + p * blocks

    def fill(c, carry):
        gap = query_block - c
        n = jnp.where((gap <= 1) & (gap >= -1), 1, 0)
        for row in named:
            n = n + jnp.where(row == c, 1, 0)
        level = jnp.full((1, rows), NEG, F32)
        for times, log in ((1, 0.0), (2, 0.6931471805599453), (3, 1.0986122886681098),
                           (4, 1.3862943611198906)):
            level = jnp.where(n == times, log, level)
        at = pl.multiple_of(lax.div(c, blocks) * slot + lax.rem(c, blocks) * BLK, 16)
        bias[pl.ds(at, BLK), :] = jnp.where(
            row_in < valid_ref[c], jnp.broadcast_to(level, (BLK, rows)), NEG
        )
        return carry

    lax.fori_loop(0, 8 * blocks, fill, 0)
    extra_row = lax.broadcasted_iota(jnp.int32, (EXTRA, rows), 0)
    for s in range(8):
        bias[s * slot + rows:(s + 1) * slot, :] = jnp.where(extra_row < n_head, 0.0, NEG)

    count = jnp.zeros((1, rows), jnp.int32)
    for b in range(blocks):
        count = jnp.where(lane_block == b, valid_ref[p * blocks + b], count)
    live_lane = lane - lane_block * BLK < count
    in_block = lax.broadcasted_iota(jnp.int32, (BLK, DH), 0)
    for b in range(blocks):
        keep = in_block < valid_ref[p * blocks + b]
        for h in range(heads):
            part = g_ref[b * BLK:(b + 1) * BLK, h * DH:(h + 1) * DH].astype(F32)
            glive[b * BLK:(b + 1) * BLK, h * DH:(h + 1) * DH] = jnp.where(
                keep, part, 0.0
            ).astype(BF16)

    scale = DH ** (-0.5)
    piece = 128
    pieces = total // piece

    def attend(h):
        cols = pl.ds(pl.multiple_of(h * DH, DH), DH)
        q = q_ref[:, cols]
        g = glive[:, cols]

        def first(j, top):
            at = pl.ds(pl.multiple_of(j * piece, piece), piece)
            key = kv[h, 0, at, :]
            s = lax.dot_general(key, q, (((1,), (1,)), ((), ())), preferred_element_type=F32)
            s = s * scale + bias[at, :]
            sbuf[at, :] = s
            kt[:, at] = key.T
            return jnp.maximum(top, jnp.max(s.reshape(piece // 8, 8, rows), axis=0))

        top = lax.fori_loop(0, pieces, first, jnp.full((8, rows), NEG, F32), unroll=True)
        top = jnp.max(top, axis=0, keepdims=True)

        def second(j, sums):
            at = pl.ds(pl.multiple_of(j * piece, piece), piece)
            value = kv[h, 1, at, :]
            e = jnp.exp(sbuf[at, :] - top)
            dp = lax.dot_general(value, g, (((1,), (1,)), ((), ())), preferred_element_type=F32)
            sbuf[at, :] = e
            dbuf[at, :] = dp
            vt[:, at] = value.T
            z, delta = sums
            z = z + jnp.sum(e.reshape(piece // 8, 8, rows), axis=0)
            delta = delta + jnp.sum((e * dp).reshape(piece // 8, 8, rows), axis=0)
            return z, delta

        zero = jnp.zeros((8, rows), F32)
        z, delta = lax.fori_loop(0, pieces, second, (zero, zero), unroll=True)
        inv = 1.0 / jnp.sum(z, axis=0, keepdims=True)
        delta = jnp.sum(delta, axis=0, keepdims=True) * inv

        def third(j, carry):
            at = pl.ds(pl.multiple_of(j * piece, piece), piece)
            prob = sbuf[at, :] * inv
            prob_b = prob.astype(BF16)
            ds = (prob * (dbuf[at, :] - delta) * scale).astype(BF16)
            pbuf[at, :] = prob_b
            dsbuf[at, :] = ds
            grads[h, 0, at, :] = jnp.dot(ds, q, preferred_element_type=F32).astype(BF16)
            grads[h, 1, at, :] = jnp.dot(prob_b, g, preferred_element_type=F32).astype(BF16)
            return carry

        lax.fori_loop(0, pieces, third, 0, unroll=True)
        out = jnp.dot(vt[...], pbuf[...], preferred_element_type=F32)
        att_ref[:, cols] = jnp.where(live_lane, out, 0.0).T.astype(BF16)
        gq = jnp.dot(kt[...], dsbuf[...], preferred_element_type=F32)
        gq_ref[:, cols] = gq.T.astype(BF16)

    def part(h, half, q):
        return grads[h, half, pl.ds(pl.multiple_of(q * slot, 16), slot), :].astype(F32)

    def keep_part(h, half, q, x):
        grads[h, half, pl.ds(pl.multiple_of(q * slot, 16), slot), :] = x.astype(BF16)

    def step(t, carry):
        @pl.when(t < heads)
        def _():
            ag(t, 0, False).wait_recv()
            ag(t, 1, False).wait_recv()
            for k in (3, 4, 5, 6):
                ag(t, k, True).start()

        @pl.when(t + 2 < heads)
        def _():
            for k in range(3):
                ag(t + 2, k, True).start()

        @pl.when((t >= 1) & (t < heads + 1))
        def _():
            ag(t - 1, 3, False).wait_recv()
            ag(t - 1, 4, False).wait_recv()
            ag(t - 1, 7, True).start()

        @pl.when((t >= 3) & (t < heads + 3))
        def _():
            h = t - 3
            for k in range(4):
                rs(h, k).wait_recv()
            for half in range(2):
                keep_part(h, half, nd, part(h, half, nd) + rsib[h, 3, half].astype(F32))
            rs(h, 4).start()
            rs(h, 5).start()

        @pl.when((t >= 4) & (t < heads + 4))
        def _():
            h = t - 4
            rs(h, 4).wait_recv()
            rs(h, 5).wait_recv()
            for k, q, half_in in ((1, nx, 1), (2, ny, 0)):
                for half in range(2):
                    x = part(h, half, q) + rsib[h, k, half].astype(F32)
                    if half == half_in:
                        x = x + rdiag[h, half].astype(F32)
                    keep_part(h, half, q, x)
                rs(h, 5 + k).start()

        @pl.when((t >= 2) & (t < heads + 2))
        def _():
            h = t - 2
            for k in (2, 5, 6, 7):
                ag(h, k, False).wait_recv()
            attend(h)
            for k in range(4):
                rs(h, k).start()

        @pl.when(t >= 5)
        def _():
            h = t - 5
            rs(h, 6).wait_recv()
            rs(h, 7).wait_recv()
            cols = pl.ds(pl.multiple_of(h * DH, DH), DH)
            for half, ref in ((0, gk_ref), (1, gv_ref)):
                x = part(h, half, p) + rsib[h, 0, half].astype(F32)
                x = x + rdir[h, 0, half].astype(F32) + rdir[h, 1, half].astype(F32)
                ref[:, cols] = x[:rows].astype(BF16)
                sc_stage[h, half] = x[rows:]

        return carry

    lax.fori_loop(0, heads + 5, step, 0)

    sc_send[...] = jnp.zeros_like(sc_send)
    for h in range(heads):
        for half in range(2):
            for t in range(n_head):
                row = half * 8 + h
                sc_send[t, row:row + 1, :] = sc_stage[h, half, t:t + 1, :]
    for d in range(1, n_head):
        scene(d, sc_send, sg_ref, sg_ssem, sg_rsem).start()
    sg_ref[hd] = sc_send[hd]
    for d in range(1, n_head):
        scene(d, sc_send, sg_ref, sg_ssem, sg_rsem).wait()

    def drain(h, carry):
        for k in range(8):
            ag(h, k, True).wait_send()
            rs(h, k).wait_send()
        return carry

    lax.fori_loop(0, heads, drain, 0)


def fused_device(queries, keys, values, grad_out, scene_keys, scene_values, valid, pattern):
    n_head = lax.axis_size("head")
    rows, features = queries.shape
    heads = features // DH
    blocks = rows // BLK
    slot = rows + EXTRA
    total = 8 * slot

    def tile(x):
        x = x.astype(F32).reshape(n_head, heads, DH)
        return jnp.pad(x, ((0, 0), (0, 8 - heads), (0, 0)))

    scene = jnp.concatenate([tile(scene_keys), tile(scene_values)], axis=1)
    vmem = pl.BlockSpec(memory_space=pltpu.VMEM)
    smem = pl.BlockSpec(memory_space=pltpu.SMEM)
    wide = jax.ShapeDtypeStruct((rows, features), BF16)
    dma = pltpu.SemaphoreType.DMA
    out = pl.pallas_call(
        functools.partial(fused_kernel, heads, n_head, blocks),
        out_shape=[wide] * 4 + [jax.ShapeDtypeStruct((n_head, 16, DH), F32)],
        in_specs=[smem, smem] + [vmem] * 5,
        out_specs=[vmem] * 5,
        scratch_shapes=[
            pltpu.VMEM((heads, 2, total, DH), BF16),
            pltpu.VMEM((heads, 2, total, DH), BF16),
            pltpu.VMEM((heads, 4, 2, slot, DH), BF16),
            pltpu.VMEM((heads, 2, slot, DH), BF16),
            pltpu.VMEM((heads, 2, 2, slot, DH), BF16),
            pltpu.VMEM((total, rows), F32),
            pltpu.VMEM((total, rows), F32),
            pltpu.VMEM((total, rows), F32),
            pltpu.VMEM((total, rows), BF16),
            pltpu.VMEM((total, rows), BF16),
            pltpu.VMEM((DH, total), BF16),
            pltpu.VMEM((DH, total), BF16),
            pltpu.VMEM((rows, features), BF16),
            pltpu.VMEM((n_head, 16, DH), F32),
            pltpu.VMEM((heads, 2, EXTRA, DH), F32),
            pltpu.VMEM((n_head, 16, DH), F32),
            dma((heads, 8)), dma((heads, 8)), dma((heads, 8)), dma((heads, 8)),
            dma((n_head,)), dma((n_head,)), dma((n_head,)), dma((n_head,)),
        ],
        compiler_params=pltpu.CompilerParams(
            collective_id=0, has_side_effects=True, vmem_limit_bytes=52 * 1024 * 1024
        ),
    )(valid, pattern, queries, keys, values, grad_out, scene)
    att, gq, gk, gv, sg = out
    gsk = sg[:, :heads].reshape(1, n_head * features).astype(BF16)
    gsv = sg[:, 8:8 + heads].reshape(1, n_head * features).astype(BF16)
    return att, gq, gk, gv, gsk, gsv


def solution(mesh):
    placed = (
        P("seq", "head"),
        P("seq", "head"),
        P("seq", "head"),
        P("seq", "head"),
        P(("seq", "head"), None),
        P(("seq", "head"), None),
        P(),
        P(),
    )
    body = fused_device if mesh.shape["seq"] == 8 else per_device
    return jax.shard_map(
        body,
        mesh=mesh,
        in_specs=placed,
        out_specs=(
            P("seq", "head"),
            P("seq", "head"),
            P("seq", "head"),
            P("seq", "head"),
            P(("seq", "head"), None),
            P(("seq", "head"), None),
        ),
        check_vma=False,
    )
```

```python
import functools

import jax
import jax.numpy as jnp
from jax import lax
from jax.experimental import pallas as pl
from jax.experimental.pallas import tpu as pltpu
from jax.sharding import PartitionSpec as P

DH = 128
BLK = 64
RAND = 3


def extended_2(block, sides, width):
    for axis, dim in sides:
        count = lax.axis_size(axis)
        forward = [(i, i + 1) for i in range(count - 1)]
        backward = [(target, source) for source, target in forward]
        low = lax.ppermute(
            lax.slice_in_dim(block, block.shape[dim] - width, None, axis=dim), axis, forward
        )
        high = lax.ppermute(lax.slice_in_dim(block, 0, width, axis=dim), axis, backward)
        block = jnp.concatenate([low, block, high], axis=dim)
    return block


def passed_along(x, axis, by):
    length = lax.axis_size(axis)
    pairs = [(i, i + by) for i in range(length) if 0 <= i + by < length]
    return lax.ppermute(x, axis, pairs)


def block_terms(query, all_keys, all_values, key_live, query_live, grad_out):
    scale = DH ** (-0.5)
    scores = (
        jnp.einsum("gqhd,gkhd->ghqk", query, all_keys, preferred_element_type=jnp.float32) * scale
    )
    scores = jnp.where(key_live[:, None, None, :], scores, -1e30)
    highest = jnp.max(scores, axis=3, keepdims=True)
    expo = jnp.exp(scores - highest)
    prob = expo / jnp.sum(expo, axis=3, keepdims=True)
    prob_round = prob.astype(jnp.bfloat16)
    live_rows = query_live[:, :, None, None]
    attended = jnp.einsum(
        "ghqk,gkhd->gqhd", prob_round, all_values, preferred_element_type=jnp.float32
    )
    attended = jnp.where(live_rows, attended, 0.0).astype(jnp.bfloat16)
    grad_live = jnp.where(live_rows, grad_out, 0.0)
    dprob = jnp.einsum("gqhd,gkhd->ghqk", grad_live, all_values, preferred_element_type=jnp.float32)
    delta = jnp.sum(prob * dprob, axis=3, keepdims=True)
    dscore = (prob * (dprob - delta) * scale).astype(jnp.bfloat16)
    grad_query = jnp.einsum("ghqk,gkhd->gqhd", dscore, all_keys, preferred_element_type=jnp.float32)
    grad_k = jnp.einsum("ghqk,gqhd->gkhd", dscore, query, preferred_element_type=jnp.float32)
    grad_v = jnp.einsum(
        "ghqk,gqhd->gkhd", prob_round, grad_live, preferred_element_type=jnp.float32
    )
    return (attended, grad_query.astype(jnp.bfloat16), grad_k, grad_v)


def per_device(queries, keys, values, grad_out, scene_keys, scene_values, valid, pattern):
    seq_count = lax.axis_size("seq")
    position = lax.axis_index("seq")
    features = queries.shape[1]
    head_count = features // DH
    blocks_dev = queries.shape[0] // BLK
    group_size = min(8, blocks_dev)
    requests = blocks_dev * RAND
    slot_count = (requests + seq_count - 2) // (seq_count - 1)
    offsets = jnp.arange(BLK, dtype=jnp.int32)
    near_count = (3 + RAND) * BLK
    parted = (
        lax.all_to_all(scene_keys, "head", split_axis=1, concat_axis=0, tiled=True),
        lax.all_to_all(scene_values, "head", split_axis=1, concat_axis=0, tiled=True),
    )
    scene_k, scene_v = (
        lax.all_gather(parted[0], "seq", axis=0, tiled=True),
        lax.all_gather(parted[1], "seq", axis=0, tiled=True),
    )
    scene_rows_all = scene_k.shape[0]
    scene_kv = jnp.stack([scene_k, scene_v]).reshape(2, 1, scene_rows_all, head_count, DH)
    scene_kv = jnp.broadcast_to(scene_kv, (2, group_size, scene_rows_all, head_count, DH))
    stacked = jnp.stack([keys, values])
    extended = extended_2(stacked, (("seq", 1),), BLK)
    all_requests = pattern.reshape(seq_count, requests)
    source = all_requests // blocks_dev
    local_block = all_requests % blocks_dev
    from_here = source == position
    send_rank = jnp.cumsum(from_here.astype(jnp.int32), axis=1) - 1
    slot_ids = jnp.arange(slot_count, dtype=jnp.int32)
    marked = from_here[:, :, None] & (send_rank[:, :, None] == slot_ids[None, None, :])
    chosen = jnp.sum(jnp.where(marked, local_block[:, :, None], 0), axis=1)
    block_view = stacked.reshape(2, blocks_dev, BLK, features)
    outgoing = block_view[:, chosen]
    incoming = lax.all_to_all(outgoing, "seq", split_axis=1, concat_axis=1, tiled=True)
    own_requests = lax.dynamic_slice_in_dim(pattern, position * blocks_dev, blocks_dev, 0).reshape(
        requests
    )
    own_source = own_requests // blocks_dev
    earlier = jnp.tril(jnp.ones((requests, requests), jnp.bool_), -1)
    same_source = own_source[:, None] == own_source[None, :]
    recv_rank = jnp.sum((same_source & earlier).astype(jnp.int32), axis=1)
    recv_place = own_source * slot_count + recv_rank
    far_blocks = incoming.reshape(2, seq_count * slot_count, BLK, features)[:, recv_place]
    far_blocks = far_blocks.reshape(2, blocks_dev, RAND, BLK, features)
    padded_valid = jnp.concatenate([jnp.zeros((1,), jnp.int32), valid, jnp.zeros((1,), jnp.int32)])
    window_count = lax.dynamic_slice_in_dim(padded_valid, position * blocks_dev, blocks_dev + 2, 0)
    far_count = valid[own_requests].reshape(blocks_dev, RAND)
    query_count = lax.dynamic_slice_in_dim(valid, position * blocks_dev, blocks_dev, 0)
    scene_live = jnp.ones((group_size, scene_rows_all), jnp.bool_)
    ext_grad = jnp.zeros((2, blocks_dev + 2, BLK, features), jnp.float32)
    query_grp = queries.reshape(group_size, BLK, head_count, DH)
    grad_grp = grad_out.reshape(group_size, BLK, head_count, DH)
    window = extended.reshape(2, group_size + 2, BLK, features)
    near_kv = jnp.concatenate(
        [
            window[:, 0:group_size, None],
            window[:, 1 : group_size + 1, None],
            window[:, 2:, None],
            far_blocks,
        ],
        axis=2,
    )
    near_kv = near_kv.reshape(2, group_size, near_count, head_count, DH)
    joined_kv = jnp.concatenate([near_kv, scene_kv], axis=2)
    counts = jnp.concatenate(
        [
            window_count[0:group_size, None],
            window_count[1 : group_size + 1, None],
            window_count[2 : group_size + 2, None],
            far_count,
        ],
        axis=1,
    )
    near_live = (offsets[None, None, :] < counts[:, :, None]).reshape(group_size, near_count)
    key_live = jnp.concatenate([near_live, scene_live], axis=1)
    query_live = offsets[None, :] < query_count[0:group_size, None]
    attended, grad_query, grad_k, grad_v = block_terms(
        query_grp, joined_kv[0], joined_kv[1], key_live, query_live, grad_grp
    )
    both_grad = jnp.stack([grad_k, grad_v])
    near_grad = both_grad[:, :, :near_count].reshape(2, group_size, 3 + RAND, BLK, features)
    scene_grad = jnp.sum(both_grad[:, :, near_count:], axis=1)
    ext_grad = ext_grad.at[:, 0:group_size].add(near_grad[:, :, 0])
    ext_grad = ext_grad.at[:, 1 : group_size + 1].add(near_grad[:, :, 1])
    ext_grad = ext_grad.at[:, 2 : group_size + 2].add(near_grad[:, :, 2])
    random_parts = near_grad[:, :, 3:].astype(jnp.bfloat16)
    attended_parts = attended.reshape(group_size * BLK, features)
    query_parts = grad_query.reshape(group_size * BLK, features)
    random_terms = random_parts.reshape(2, requests, BLK, features)
    outgoing_grad = (
        jnp.zeros((2, seq_count * slot_count, BLK, features), jnp.bfloat16)
        .at[:, recv_place]
        .set(random_terms)
    )
    outgoing_grad = outgoing_grad.reshape(2, seq_count, slot_count, BLK, features)
    returned = lax.all_to_all(outgoing_grad, "seq", split_axis=1, concat_axis=1, tiled=True)
    selector = (
        chosen.reshape(-1)[:, None] == jnp.arange(blocks_dev, dtype=jnp.int32)[None, :]
    ).astype(jnp.bfloat16)
    gathered_grad = jnp.einsum(
        "sb,xsk->xbk",
        selector,
        returned.reshape(2, seq_count * slot_count, BLK * features),
        preferred_element_type=jnp.float32,
    )
    from_right = passed_along(ext_grad[:, 0].astype(jnp.bfloat16), "seq", -1).astype(jnp.float32)
    from_left = passed_along(ext_grad[:, blocks_dev + 1].astype(jnp.bfloat16), "seq", 1).astype(
        jnp.float32
    )
    inner = ext_grad[:, 1 : blocks_dev + 1]
    inner = inner.at[:, blocks_dev - 1].add(from_right).at[:, 0].add(from_left)
    total_grad = inner.reshape(2, blocks_dev, BLK * features) + gathered_grad
    grad_keys = total_grad[0].reshape(blocks_dev * BLK, features).astype(jnp.bfloat16)
    grad_values = total_grad[1].reshape(blocks_dev * BLK, features).astype(jnp.bfloat16)
    scene_terms_k = scene_grad[0].reshape(scene_rows_all, features)
    scene_terms_v = scene_grad[1].reshape(scene_rows_all, features)
    mine_k, mine_v = (
        lax.psum_scatter(scene_terms_k, "seq", scatter_dimension=0, tiled=True),
        lax.psum_scatter(scene_terms_v, "seq", scatter_dimension=0, tiled=True),
    )
    back_k, back_v = (
        lax.all_to_all(mine_k, "head", split_axis=0, concat_axis=1, tiled=True),
        lax.all_to_all(mine_v, "head", split_axis=0, concat_axis=1, tiled=True),
    )
    return (
        attended_parts,
        query_parts,
        grad_keys,
        grad_values,
        back_k.astype(jnp.bfloat16),
        back_v.astype(jnp.bfloat16),
    )


NEG = -1e30
SCENE_ROWS = 128
MESH = pl.DeviceIdType.MESH
F32 = jnp.float32
BF16 = jnp.bfloat16


def fused_kernel(
    heads, n_head, blocks,
    valid_ref, pattern_ref, q_ref, k_ref, v_ref, g_ref, sk_ref, sv_ref,
    att_ref, gq_ref, gk_ref, gv_ref, sg_ref,
    kv, grads, rsib, rdiag, rdir, bias, sbuf, dbuf, pbuf, dsbuf, kt, vt, glive,
    sc_src, sc_recv, sc_send, scx, sc_all, scg, srsib, srdiag, srdir,
    ag_send, ag_recv, rs_send, rs_recv, sc_ssem, sc_rsem, sg_ssem, sg_rsem,
    sx_send, sx_recv, sr_send, sr_recv,
):
    rows = blocks * BLK
    slot = rows
    base = 8 * slot
    total = base + SCENE_ROWS
    tokens = 8 * n_head
    p = lax.axis_index("seq")
    hd = lax.axis_index("head")
    nc = p + 1 - 2 * lax.rem(p, 2)
    nx = p + 2 - 4 * lax.rem(lax.div(p, 2), 2)
    ny = p + 4 - 8 * lax.rem(lax.div(p, 4), 2)
    nd = nx + ny - p
    flip = nc - p
    own = pl.multiple_of(p * slot, 16)

    def pack(h):
        kv[h, 0, pl.ds(own, rows), :] = k_ref[:, h * DH:(h + 1) * DH]
        kv[h, 1, pl.ds(own, rows), :] = v_ref[:, h * DH:(h + 1) * DH]

    barrier = pltpu.get_barrier_semaphore()
    for target in (nc, nx, ny):
        pl.semaphore_signal(barrier, inc=1, device_id={"seq": target}, device_id_type=MESH)
    for d in range(1, n_head):
        pl.semaphore_signal(
            barrier, inc=1, device_id={"head": lax.rem(hd + d, n_head)}, device_id_type=MESH
        )
    for h in range(min(2, heads)):
        pack(h)
    sc_src[...] = jnp.zeros_like(sc_src)
    for t in range(n_head):
        for h in range(heads):
            at = (t * heads + h) * DH
            sc_src[t, h:h + 1, :] = sk_ref[:, at:at + DH].astype(F32)
            sc_src[t, 8 + h:9 + h, :] = sv_ref[:, at:at + DH].astype(F32)
    pl.semaphore_wait(barrier, 3 + n_head - 1)

    def at_slot(ref, h, q):
        return ref.at[h, :, pl.ds(pl.multiple_of(q * slot, 16), slot), :]

    def at_half(ref, h, half, q):
        return ref.at[h, half, pl.ds(pl.multiple_of(q * slot, 16), slot), :]

    def copy(src, dst, ssem, rsem, dev):
        return pltpu.make_async_remote_copy(
            src_ref=src, dst_ref=dst, send_sem=ssem, recv_sem=rsem,
            device_id={"seq": dev}, device_id_type=MESH,
        )

    def ag(h, k, sending):
        sent, dev, arrives = (
            (p, nx, nx), (p, ny, ny), (p, nc, nc), (nx, ny, nd), (ny, nx, nd),
            (nx, nc, nx + flip), (ny, nc, ny + flip), (nd, nc, nd + flip),
        )[k]
        s = sent if sending else arrives
        ref = at_half(kv, h, k - 3, s) if k in (3, 4) else at_slot(kv, h, s)
        return copy(ref, ref, ag_send.at[h, k], ag_recv.at[h, k], dev)

    def rs(h, k):
        if k < 4:
            q = (p, nx, ny, nd)[k] + flip
            src, dst, dev = at_slot(grads, h, q), rsib.at[h, k], nc
        elif k < 6:
            src, dst = at_half(grads, h, k - 4, nd), rdiag.at[h, k - 4]
            dev = (nx, ny)[k - 4]
        else:
            dev = (nx, ny)[k - 6]
            src, dst = at_slot(grads, h, dev), rdir.at[h, k - 6]
        return copy(src, dst, rs_send.at[h, k], rs_recv.at[h, k], dev)

    def scene(d, src, dst, ssem, rsem):
        target = lax.rem(hd + d, n_head)
        return pltpu.make_async_remote_copy(
            src_ref=src.at[target], dst_ref=dst.at[hd], send_sem=ssem.at[d], recv_sem=rsem.at[d],
            device_id={"head": target}, device_id_type=MESH,
        )

    def scene_gather(k, sending):
        sent, dev, arrives = (
            (p, nx, nx), (p, ny, ny), (p, nc, nc), (nx, ny, nd),
            (nx, nc, nx + flip), (ny, nc, ny + flip), (nd, nc, nd + flip),
        )[k]
        ref = scx.at[sent if sending else arrives]
        return copy(ref, ref, sx_send.at[k], sx_recv.at[k], dev)

    def scene_sum(k):
        src, dst, dev = (
            (nc, srsib.at[0], nc), (nx + flip, srsib.at[1], nc), (ny + flip, srsib.at[2], nc),
            (nd + flip, srsib.at[3], nc), (nd, srdiag, nx), (nx, srdir.at[0], nx),
            (ny, srdir.at[1], ny),
        )[k]
        return copy(scg.at[src], dst, sr_send.at[k], sr_recv.at[k], dev)

    def scene_row(h, half):
        return (half * heads + h) * n_head

    for d in range(1, n_head):
        scene(d, sc_src, sc_recv, sc_ssem, sc_rsem).start()
    for h in range(min(2, heads)):
        for k in range(3):
            ag(h, k, True).start()
    sc_recv[hd] = sc_src[hd]
    for h in range(2, heads):
        pack(h)
    for d in range(1, n_head):
        scene(d, sc_src, sc_recv, sc_ssem, sc_rsem).wait()
    for h in range(heads):
        for half in range(2):
            for t in range(n_head):
                row = half * 8 + h
                at = scene_row(h, half) + t
                scx[p, at:at + 1, :] = sc_recv[t, row:row + 1, :]
    for k in range(3):
        scene_gather(k, True).start()

    lane = lax.broadcasted_iota(jnp.int32, (1, rows), 1)
    lane_block = lax.div(lane, BLK)
    row_in = lax.broadcasted_iota(jnp.int32, (BLK, rows), 0)
    named = []
    for r in range(RAND):
        row = jnp.zeros((1, rows), jnp.int32)
        for b in range(blocks):
            row = jnp.where(lane_block == b, pattern_ref[p * blocks + b, r], row)
        named.append(row)
    query_block = lane_block + p * blocks

    def fill(c, carry):
        gap = query_block - c
        n = jnp.where((gap <= 1) & (gap >= -1), 1, 0)
        for row in named:
            n = n + jnp.where(row == c, 1, 0)
        level = jnp.full((1, rows), NEG, F32)
        for times, log in ((1, 0.0), (2, 0.6931471805599453), (3, 1.0986122886681098),
                           (4, 1.3862943611198906)):
            level = jnp.where(n == times, log, level)
        at = pl.multiple_of(c * BLK, BLK)
        bias[pl.ds(at, BLK), :] = jnp.where(
            row_in < valid_ref[c], jnp.broadcast_to(level, (BLK, rows)), NEG
        )
        return carry

    lax.fori_loop(0, 8 * blocks, fill, 0)
    scene_gather(0, False).wait_recv()
    scene_gather(1, False).wait_recv()
    for k in (3, 4, 5):
        scene_gather(k, True).start()
    extra_row = lax.broadcasted_iota(jnp.int32, (SCENE_ROWS, rows), 0)
    bias[base:, :] = jnp.where(extra_row < tokens, 0.0, NEG)
    for h in range(heads):
        for half in range(2):
            kv[h, half, base + tokens:, :] = jnp.zeros((SCENE_ROWS - tokens, DH), BF16)

    count = jnp.zeros((1, rows), jnp.int32)
    for b in range(blocks):
        count = jnp.where(lane_block == b, valid_ref[p * blocks + b], count)
    live_lane = lane - lane_block * BLK < count
    in_block = lax.broadcasted_iota(jnp.int32, (BLK, DH), 0)
    for b in range(blocks):
        keep = in_block < valid_ref[p * blocks + b]
        for h in range(heads):
            part = g_ref[b * BLK:(b + 1) * BLK, h * DH:(h + 1) * DH].astype(F32)
            glive[b * BLK:(b + 1) * BLK, h * DH:(h + 1) * DH] = jnp.where(
                keep, part, 0.0
            ).astype(BF16)

    scene_gather(3, False).wait_recv()
    scene_gather(6, True).start()
    for k in (2, 4, 5, 6):
        scene_gather(k, False).wait_recv()
    for h in range(heads):
        for half in range(2):
            for i in range(8):
                at = scene_row(h, half)
                sc_all[h, half, i * n_head:(i + 1) * n_head, :] = scx[i, at:at + n_head, :]
            kv[h, half, base:base + tokens, :] = sc_all[h, half].astype(BF16)

    scale = DH ** (-0.5)
    piece = SCENE_ROWS
    pieces = total // piece

    def attend(h):
        cols = pl.ds(pl.multiple_of(h * DH, DH), DH)
        q = q_ref[:, cols]
        g = glive[:, cols]

        def first(j, top):
            at = pl.ds(pl.multiple_of(j * piece, piece), piece)
            key = kv[h, 0, at, :]
            s = lax.dot_general(key, q, (((1,), (1,)), ((), ())), preferred_element_type=F32)
            s = s * scale + bias[at, :]
            sbuf[at, :] = s
            kt[:, at] = key.T
            return jnp.maximum(top, jnp.max(s.reshape(piece // 8, 8, rows), axis=0))

        top = lax.fori_loop(0, pieces, first, jnp.full((8, rows), NEG, F32), unroll=True)
        top = jnp.max(top, axis=0, keepdims=True)

        def second(j, sums):
            at = pl.ds(pl.multiple_of(j * piece, piece), piece)
            value = kv[h, 1, at, :]
            e = jnp.exp(sbuf[at, :] - top)
            dp = lax.dot_general(value, g, (((1,), (1,)), ((), ())), preferred_element_type=F32)
            sbuf[at, :] = e
            dbuf[at, :] = dp
            vt[:, at] = value.T
            z, delta = sums
            z = z + jnp.sum(e.reshape(piece // 8, 8, rows), axis=0)
            delta = delta + jnp.sum((e * dp).reshape(piece // 8, 8, rows), axis=0)
            return z, delta

        zero = jnp.zeros((8, rows), F32)
        z, delta = lax.fori_loop(0, pieces, second, (zero, zero), unroll=True)
        inv = 1.0 / jnp.sum(z, axis=0, keepdims=True)
        delta = jnp.sum(delta, axis=0, keepdims=True) * inv

        def terms(j):
            at = pl.ds(pl.multiple_of(j * piece, piece), piece)
            prob = sbuf[at, :] * inv
            prob_b = prob.astype(BF16)
            ds = (prob * (dbuf[at, :] - delta) * scale).astype(BF16)
            pbuf[at, :] = prob_b
            dsbuf[at, :] = ds
            grad_k = jnp.dot(ds, q, preferred_element_type=F32)
            grad_v = jnp.dot(prob_b, g, preferred_element_type=F32)
            return at, grad_k, grad_v

        def third(j, carry):
            at, grad_k, grad_v = terms(j)
            grads[h, 0, at, :] = grad_k.astype(BF16)
            grads[h, 1, at, :] = grad_v.astype(BF16)
            return carry

        lax.fori_loop(0, pieces - 1, third, 0, unroll=True)
        _, grad_k, grad_v = terms(pieces - 1)
        sc_all[h, 0] = grad_k[:tokens]
        sc_all[h, 1] = grad_v[:tokens]
        out = jnp.dot(vt[...], pbuf[...], preferred_element_type=F32)
        att_ref[:, cols] = jnp.where(live_lane, out, 0.0).T.astype(BF16)
        gq = jnp.dot(kt[...], dsbuf[...], preferred_element_type=F32)
        gq_ref[:, cols] = gq.T.astype(BF16)

    def part(h, half, q):
        return grads[h, half, pl.ds(pl.multiple_of(q * slot, 16), slot), :].astype(F32)

    def keep_part(h, half, q, x):
        grads[h, half, pl.ds(pl.multiple_of(q * slot, 16), slot), :] = x.astype(BF16)

    def step(t, carry):
        @pl.when(t < heads)
        def _():
            ag(t, 0, False).wait_recv()
            ag(t, 1, False).wait_recv()
            for k in (3, 4, 5, 6):
                ag(t, k, True).start()

        @pl.when(t + 2 < heads)
        def _():
            for k in range(3):
                ag(t + 2, k, True).start()

        @pl.when((t >= 1) & (t < heads + 1))
        def _():
            ag(t - 1, 3, False).wait_recv()
            ag(t - 1, 4, False).wait_recv()
            ag(t - 1, 7, True).start()

        @pl.when((t >= 3) & (t < heads + 3))
        def _():
            h = t - 3
            for k in range(4):
                rs(h, k).wait_recv()
            for half in range(2):
                keep_part(h, half, nd, part(h, half, nd) + rsib[h, 3, half].astype(F32))
            rs(h, 4).start()
            rs(h, 5).start()

        @pl.when((t >= 4) & (t < heads + 4))
        def _():
            h = t - 4
            rs(h, 4).wait_recv()
            rs(h, 5).wait_recv()
            for k, q, half_in in ((1, nx, 1), (2, ny, 0)):
                for half in range(2):
                    x = part(h, half, q) + rsib[h, k, half].astype(F32)
                    if half == half_in:
                        x = x + rdiag[h, half].astype(F32)
                    keep_part(h, half, q, x)
                rs(h, 5 + k).start()

        @pl.when((t >= 2) & (t < heads + 2))
        def _():
            h = t - 2
            for k in (2, 5, 6, 7):
                ag(h, k, False).wait_recv()
            attend(h)
            for k in range(4):
                rs(h, k).start()

        @pl.when(t >= 5)
        def _():
            h = t - 5
            rs(h, 6).wait_recv()
            rs(h, 7).wait_recv()
            cols = pl.ds(pl.multiple_of(h * DH, DH), DH)
            for half, ref in ((0, gk_ref), (1, gv_ref)):
                x = part(h, half, p) + rsib[h, 0, half].astype(F32)
                x = x + rdir[h, 0, half].astype(F32) + rdir[h, 1, half].astype(F32)
                ref[:, cols] = x.astype(BF16)

        @pl.when(t == heads + 1)
        def _():
            for h in range(heads):
                for half in range(2):
                    at = scene_row(h, half)
                    for i in range(8):
                        scg[i, at:at + n_head, :] = sc_all[
                            h, half, i * n_head:(i + 1) * n_head, :
                        ]
            for k in range(4):
                scene_sum(k).start()

        @pl.when(t == heads + 2)
        def _():
            for k in range(4):
                scene_sum(k).wait_recv()
            scg[nd] = scg[nd] + srsib[3]
            scene_sum(4).start()

        @pl.when(t == heads + 3)
        def _():
            scene_sum(4).wait_recv()
            scg[nx] = scg[nx] + srsib[1]
            scg[ny] = scg[ny] + srsib[2] + srdiag[...]
            scene_sum(5).start()
            scene_sum(6).start()

        return carry

    lax.fori_loop(0, heads + 5, step, 0)

    scene_sum(5).wait_recv()
    scene_sum(6).wait_recv()
    scg[p] = scg[p] + srsib[0] + srdir[0] + srdir[1]
    sc_send[...] = jnp.zeros_like(sc_send)
    for h in range(heads):
        for half in range(2):
            for t in range(n_head):
                row = half * 8 + h
                at = scene_row(h, half) + t
                sc_send[t, row:row + 1, :] = scg[p, at:at + 1, :]
    for d in range(1, n_head):
        scene(d, sc_send, sg_ref, sg_ssem, sg_rsem).start()
    sg_ref[hd] = sc_send[hd]
    for d in range(1, n_head):
        scene(d, sc_send, sg_ref, sg_ssem, sg_rsem).wait()

    def drain(h, carry):
        for k in range(8):
            ag(h, k, True).wait_send()
            rs(h, k).wait_send()
        return carry

    lax.fori_loop(0, heads, drain, 0)
    for k in range(7):
        scene_gather(k, True).wait_send()
        scene_sum(k).wait_send()


def finish_kernel(heads, n_head, a_ref, b_ref, c_ref, d_ref, sg_ref, ao, bo, co, do, sko, svo):
    ao[...] = a_ref[...]
    bo[...] = b_ref[...]
    co[...] = c_ref[...]
    do[...] = d_ref[...]
    for t in range(n_head):
        for h in range(heads):
            at = (t * heads + h) * DH
            sko[:, at:at + DH] = sg_ref[t, h:h + 1, :].astype(BF16)
            svo[:, at:at + DH] = sg_ref[t, 8 + h:9 + h, :].astype(BF16)


def fused_device(queries, keys, values, grad_out, scene_keys, scene_values, valid, pattern):
    n_head = lax.axis_size("head")
    rows, features = queries.shape
    heads = features // DH
    blocks = rows // BLK
    slot = rows
    base = 8 * slot
    total = base + SCENE_ROWS
    tokens = 8 * n_head
    flat = 2 * heads * n_head
    vmem = pl.BlockSpec(memory_space=pltpu.VMEM)
    smem = pl.BlockSpec(memory_space=pltpu.SMEM)
    wide = jax.ShapeDtypeStruct((rows, features), BF16)
    dma = pltpu.SemaphoreType.DMA
    out = pl.pallas_call(
        functools.partial(fused_kernel, heads, n_head, blocks),
        out_shape=[wide] * 4 + [jax.ShapeDtypeStruct((n_head, 16, DH), F32)],
        in_specs=[smem, smem] + [vmem] * 6,
        out_specs=[vmem] * 5,
        scratch_shapes=[
            pltpu.VMEM((heads, 2, total, DH), BF16),
            pltpu.VMEM((heads, 2, base, DH), BF16),
            pltpu.VMEM((heads, 4, 2, slot, DH), BF16),
            pltpu.VMEM((heads, 2, slot, DH), BF16),
            pltpu.VMEM((heads, 2, 2, slot, DH), BF16),
            pltpu.VMEM((total, rows), F32),
            pltpu.VMEM((total, rows), F32),
            pltpu.VMEM((total, rows), F32),
            pltpu.VMEM((total, rows), BF16),
            pltpu.VMEM((total, rows), BF16),
            pltpu.VMEM((DH, total), BF16),
            pltpu.VMEM((DH, total), BF16),
            pltpu.VMEM((rows, features), BF16),
            pltpu.VMEM((n_head, 16, DH), F32),
            pltpu.VMEM((n_head, 16, DH), F32),
            pltpu.VMEM((n_head, 16, DH), F32),
            pltpu.VMEM((8, flat, DH), F32),
            pltpu.VMEM((heads, 2, tokens, DH), F32),
            pltpu.VMEM((8, flat, DH), F32),
            pltpu.VMEM((4, flat, DH), F32),
            pltpu.VMEM((flat, DH), F32),
            pltpu.VMEM((2, flat, DH), F32),
            dma((heads, 8)), dma((heads, 8)), dma((heads, 8)), dma((heads, 8)),
            dma((n_head,)), dma((n_head,)), dma((n_head,)), dma((n_head,)),
            dma((7,)), dma((7,)), dma((7,)), dma((7,)),
        ],
        compiler_params=pltpu.CompilerParams(
            collective_id=0, has_side_effects=True, vmem_limit_bytes=52 * 1024 * 1024
        ),
    )(valid, pattern, queries, keys, values, grad_out, scene_keys, scene_values)
    row = jax.ShapeDtypeStruct((1, n_head * features), BF16)
    return tuple(
        pl.pallas_call(
            functools.partial(finish_kernel, heads, n_head),
            out_shape=[wide] * 4 + [row] * 2,
            in_specs=[vmem] * 5,
            out_specs=[vmem] * 6,
        )(*out)
    )


def solution(mesh):
    placed = (
        P("seq", "head"),
        P("seq", "head"),
        P("seq", "head"),
        P("seq", "head"),
        P(("seq", "head"), None),
        P(("seq", "head"), None),
        P(),
        P(),
    )
    body = fused_device if mesh.shape["seq"] == 8 else per_device
    return jax.shard_map(
        body,
        mesh=mesh,
        in_specs=placed,
        out_specs=(
            P("seq", "head"),
            P("seq", "head"),
            P("seq", "head"),
            P("seq", "head"),
            P(("seq", "head"), None),
            P(("seq", "head"), None),
        ),
        check_vma=False,
    )
```

```python
import functools

import jax
import jax.numpy as jnp
from jax import lax
from jax.experimental import pallas as pl
from jax.experimental.pallas import tpu as pltpu
from jax.sharding import PartitionSpec as P

DH = 128
BLK = 64
RAND = 3


def extended_2(block, sides, width):
    for axis, dim in sides:
        count = lax.axis_size(axis)
        forward = [(i, i + 1) for i in range(count - 1)]
        backward = [(target, source) for source, target in forward]
        low = lax.ppermute(
            lax.slice_in_dim(block, block.shape[dim] - width, None, axis=dim), axis, forward
        )
        high = lax.ppermute(lax.slice_in_dim(block, 0, width, axis=dim), axis, backward)
        block = jnp.concatenate([low, block, high], axis=dim)
    return block


def passed_along(x, axis, by):
    length = lax.axis_size(axis)
    pairs = [(i, i + by) for i in range(length) if 0 <= i + by < length]
    return lax.ppermute(x, axis, pairs)


def block_terms(query, all_keys, all_values, key_live, query_live, grad_out):
    scale = DH ** (-0.5)
    scores = (
        jnp.einsum("gqhd,gkhd->ghqk", query, all_keys, preferred_element_type=jnp.float32) * scale
    )
    scores = jnp.where(key_live[:, None, None, :], scores, -1e30)
    highest = jnp.max(scores, axis=3, keepdims=True)
    expo = jnp.exp(scores - highest)
    prob = expo / jnp.sum(expo, axis=3, keepdims=True)
    prob_round = prob.astype(jnp.bfloat16)
    live_rows = query_live[:, :, None, None]
    attended = jnp.einsum(
        "ghqk,gkhd->gqhd", prob_round, all_values, preferred_element_type=jnp.float32
    )
    attended = jnp.where(live_rows, attended, 0.0).astype(jnp.bfloat16)
    grad_live = jnp.where(live_rows, grad_out, 0.0)
    dprob = jnp.einsum("gqhd,gkhd->ghqk", grad_live, all_values, preferred_element_type=jnp.float32)
    delta = jnp.sum(prob * dprob, axis=3, keepdims=True)
    dscore = (prob * (dprob - delta) * scale).astype(jnp.bfloat16)
    grad_query = jnp.einsum("ghqk,gkhd->gqhd", dscore, all_keys, preferred_element_type=jnp.float32)
    grad_k = jnp.einsum("ghqk,gqhd->gkhd", dscore, query, preferred_element_type=jnp.float32)
    grad_v = jnp.einsum(
        "ghqk,gqhd->gkhd", prob_round, grad_live, preferred_element_type=jnp.float32
    )
    return (attended, grad_query.astype(jnp.bfloat16), grad_k, grad_v)


def per_device(queries, keys, values, grad_out, scene_keys, scene_values, valid, pattern):
    seq_count = lax.axis_size("seq")
    position = lax.axis_index("seq")
    features = queries.shape[1]
    head_count = features // DH
    blocks_dev = queries.shape[0] // BLK
    group_size = min(8, blocks_dev)
    requests = blocks_dev * RAND
    slot_count = (requests + seq_count - 2) // (seq_count - 1)
    offsets = jnp.arange(BLK, dtype=jnp.int32)
    near_count = (3 + RAND) * BLK
    parted = (
        lax.all_to_all(scene_keys, "head", split_axis=1, concat_axis=0, tiled=True),
        lax.all_to_all(scene_values, "head", split_axis=1, concat_axis=0, tiled=True),
    )
    scene_k, scene_v = (
        lax.all_gather(parted[0], "seq", axis=0, tiled=True),
        lax.all_gather(parted[1], "seq", axis=0, tiled=True),
    )
    scene_rows_all = scene_k.shape[0]
    scene_kv = jnp.stack([scene_k, scene_v]).reshape(2, 1, scene_rows_all, head_count, DH)
    scene_kv = jnp.broadcast_to(scene_kv, (2, group_size, scene_rows_all, head_count, DH))
    stacked = jnp.stack([keys, values])
    extended = extended_2(stacked, (("seq", 1),), BLK)
    all_requests = pattern.reshape(seq_count, requests)
    source = all_requests // blocks_dev
    local_block = all_requests % blocks_dev
    from_here = source == position
    send_rank = jnp.cumsum(from_here.astype(jnp.int32), axis=1) - 1
    slot_ids = jnp.arange(slot_count, dtype=jnp.int32)
    marked = from_here[:, :, None] & (send_rank[:, :, None] == slot_ids[None, None, :])
    chosen = jnp.sum(jnp.where(marked, local_block[:, :, None], 0), axis=1)
    block_view = stacked.reshape(2, blocks_dev, BLK, features)
    outgoing = block_view[:, chosen]
    incoming = lax.all_to_all(outgoing, "seq", split_axis=1, concat_axis=1, tiled=True)
    own_requests = lax.dynamic_slice_in_dim(pattern, position * blocks_dev, blocks_dev, 0).reshape(
        requests
    )
    own_source = own_requests // blocks_dev
    earlier = jnp.tril(jnp.ones((requests, requests), jnp.bool_), -1)
    same_source = own_source[:, None] == own_source[None, :]
    recv_rank = jnp.sum((same_source & earlier).astype(jnp.int32), axis=1)
    recv_place = own_source * slot_count + recv_rank
    far_blocks = incoming.reshape(2, seq_count * slot_count, BLK, features)[:, recv_place]
    far_blocks = far_blocks.reshape(2, blocks_dev, RAND, BLK, features)
    padded_valid = jnp.concatenate([jnp.zeros((1,), jnp.int32), valid, jnp.zeros((1,), jnp.int32)])
    window_count = lax.dynamic_slice_in_dim(padded_valid, position * blocks_dev, blocks_dev + 2, 0)
    far_count = valid[own_requests].reshape(blocks_dev, RAND)
    query_count = lax.dynamic_slice_in_dim(valid, position * blocks_dev, blocks_dev, 0)
    scene_live = jnp.ones((group_size, scene_rows_all), jnp.bool_)
    ext_grad = jnp.zeros((2, blocks_dev + 2, BLK, features), jnp.float32)
    query_grp = queries.reshape(group_size, BLK, head_count, DH)
    grad_grp = grad_out.reshape(group_size, BLK, head_count, DH)
    window = extended.reshape(2, group_size + 2, BLK, features)
    near_kv = jnp.concatenate(
        [
            window[:, 0:group_size, None],
            window[:, 1 : group_size + 1, None],
            window[:, 2:, None],
            far_blocks,
        ],
        axis=2,
    )
    near_kv = near_kv.reshape(2, group_size, near_count, head_count, DH)
    joined_kv = jnp.concatenate([near_kv, scene_kv], axis=2)
    counts = jnp.concatenate(
        [
            window_count[0:group_size, None],
            window_count[1 : group_size + 1, None],
            window_count[2 : group_size + 2, None],
            far_count,
        ],
        axis=1,
    )
    near_live = (offsets[None, None, :] < counts[:, :, None]).reshape(group_size, near_count)
    key_live = jnp.concatenate([near_live, scene_live], axis=1)
    query_live = offsets[None, :] < query_count[0:group_size, None]
    attended, grad_query, grad_k, grad_v = block_terms(
        query_grp, joined_kv[0], joined_kv[1], key_live, query_live, grad_grp
    )
    both_grad = jnp.stack([grad_k, grad_v])
    near_grad = both_grad[:, :, :near_count].reshape(2, group_size, 3 + RAND, BLK, features)
    scene_grad = jnp.sum(both_grad[:, :, near_count:], axis=1)
    ext_grad = ext_grad.at[:, 0:group_size].add(near_grad[:, :, 0])
    ext_grad = ext_grad.at[:, 1 : group_size + 1].add(near_grad[:, :, 1])
    ext_grad = ext_grad.at[:, 2 : group_size + 2].add(near_grad[:, :, 2])
    random_parts = near_grad[:, :, 3:].astype(jnp.bfloat16)
    attended_parts = attended.reshape(group_size * BLK, features)
    query_parts = grad_query.reshape(group_size * BLK, features)
    random_terms = random_parts.reshape(2, requests, BLK, features)
    outgoing_grad = (
        jnp.zeros((2, seq_count * slot_count, BLK, features), jnp.bfloat16)
        .at[:, recv_place]
        .set(random_terms)
    )
    outgoing_grad = outgoing_grad.reshape(2, seq_count, slot_count, BLK, features)
    returned = lax.all_to_all(outgoing_grad, "seq", split_axis=1, concat_axis=1, tiled=True)
    selector = (
        chosen.reshape(-1)[:, None] == jnp.arange(blocks_dev, dtype=jnp.int32)[None, :]
    ).astype(jnp.bfloat16)
    gathered_grad = jnp.einsum(
        "sb,xsk->xbk",
        selector,
        returned.reshape(2, seq_count * slot_count, BLK * features),
        preferred_element_type=jnp.float32,
    )
    from_right = passed_along(ext_grad[:, 0].astype(jnp.bfloat16), "seq", -1).astype(jnp.float32)
    from_left = passed_along(ext_grad[:, blocks_dev + 1].astype(jnp.bfloat16), "seq", 1).astype(
        jnp.float32
    )
    inner = ext_grad[:, 1 : blocks_dev + 1]
    inner = inner.at[:, blocks_dev - 1].add(from_right).at[:, 0].add(from_left)
    total_grad = inner.reshape(2, blocks_dev, BLK * features) + gathered_grad
    grad_keys = total_grad[0].reshape(blocks_dev * BLK, features).astype(jnp.bfloat16)
    grad_values = total_grad[1].reshape(blocks_dev * BLK, features).astype(jnp.bfloat16)
    scene_terms_k = scene_grad[0].reshape(scene_rows_all, features)
    scene_terms_v = scene_grad[1].reshape(scene_rows_all, features)
    mine_k, mine_v = (
        lax.psum_scatter(scene_terms_k, "seq", scatter_dimension=0, tiled=True),
        lax.psum_scatter(scene_terms_v, "seq", scatter_dimension=0, tiled=True),
    )
    back_k, back_v = (
        lax.all_to_all(mine_k, "head", split_axis=0, concat_axis=1, tiled=True),
        lax.all_to_all(mine_v, "head", split_axis=0, concat_axis=1, tiled=True),
    )
    return (
        attended_parts,
        query_parts,
        grad_keys,
        grad_values,
        back_k.astype(jnp.bfloat16),
        back_v.astype(jnp.bfloat16),
    )


NEG = -1e30
SCENE_ROWS = 128
MESH = pl.DeviceIdType.MESH
F32 = jnp.float32
BF16 = jnp.bfloat16


def fused_kernel(
    heads, n_head, blocks,
    valid_ref, pattern_ref, q_ref, k_ref, v_ref, g_ref, sk_ref, sv_ref,
    att_ref, gq_ref, gk_ref, gv_ref, sg_ref,
    kv, grads, rsib, rdiag, rdir, bias, sbuf, dbuf, pbuf, dsbuf, kt, vt, glive, qt, gt,
    sc_src, sc_recv, sc_send, scx, sc_all, scg, srsib, srdiag, srdir,
    ag_send, ag_recv, rs_send, rs_recv, sc_ssem, sc_rsem, sg_ssem, sg_rsem,
    sx_send, sx_recv, sr_send, sr_recv,
):
    rows = blocks * BLK
    slot = rows
    base = 8 * slot
    total = base + SCENE_ROWS
    tokens = 8 * n_head
    p = lax.axis_index("seq")
    hd = lax.axis_index("head")
    nc = p + 1 - 2 * lax.rem(p, 2)
    nx = p + 2 - 4 * lax.rem(lax.div(p, 2), 2)
    ny = p + 4 - 8 * lax.rem(lax.div(p, 4), 2)
    nd = nx + ny - p
    flip = nc - p
    own = pl.multiple_of(p * slot, 16)

    def pack(h):
        kv[h, 0, pl.ds(own, rows), :] = k_ref[:, h * DH:(h + 1) * DH]
        kv[h, 1, pl.ds(own, rows), :] = v_ref[:, h * DH:(h + 1) * DH]

    barrier = pltpu.get_barrier_semaphore()
    for target in (nc, nx, ny):
        pl.semaphore_signal(barrier, inc=1, device_id={"seq": target}, device_id_type=MESH)
    for d in range(1, n_head):
        pl.semaphore_signal(
            barrier, inc=1, device_id={"head": lax.rem(hd + d, n_head)}, device_id_type=MESH
        )
    for h in range(min(2, heads)):
        pack(h)
    sc_src[...] = jnp.zeros_like(sc_src)
    for t in range(n_head):
        for h in range(heads):
            at = (t * heads + h) * DH
            sc_src[t, h:h + 1, :] = sk_ref[:, at:at + DH].astype(F32)
            sc_src[t, 8 + h:9 + h, :] = sv_ref[:, at:at + DH].astype(F32)
    pl.semaphore_wait(barrier, 3 + n_head - 1)

    def at_slot(ref, h, q):
        return ref.at[h, :, pl.ds(pl.multiple_of(q * slot, 16), slot), :]

    def at_half(ref, h, half, q):
        return ref.at[h, half, pl.ds(pl.multiple_of(q * slot, 16), slot), :]

    def copy(src, dst, ssem, rsem, dev):
        return pltpu.make_async_remote_copy(
            src_ref=src, dst_ref=dst, send_sem=ssem, recv_sem=rsem,
            device_id={"seq": dev}, device_id_type=MESH,
        )

    def ag(h, k, sending):
        sent, dev, arrives = (
            (p, nx, nx), (p, ny, ny), (p, nc, nc), (nx, ny, nd), (ny, nx, nd),
            (nx, nc, nx + flip), (ny, nc, ny + flip), (nd, nc, nd + flip),
        )[k]
        s = sent if sending else arrives
        ref = at_half(kv, h, k - 3, s) if k in (3, 4) else at_slot(kv, h, s)
        return copy(ref, ref, ag_send.at[h, k], ag_recv.at[h, k], dev)

    def rs(h, k):
        if k < 4:
            q = (p, nx, ny, nd)[k] + flip
            src, dst, dev = at_slot(grads, h, q), rsib.at[h, k], nc
        elif k < 6:
            src, dst = at_half(grads, h, k - 4, nd), rdiag.at[h, k - 4]
            dev = (nx, ny)[k - 4]
        else:
            dev = (nx, ny)[k - 6]
            src, dst = at_slot(grads, h, dev), rdir.at[h, k - 6]
        return copy(src, dst, rs_send.at[h, k], rs_recv.at[h, k], dev)

    def scene(d, src, dst, ssem, rsem):
        target = lax.rem(hd + d, n_head)
        return pltpu.make_async_remote_copy(
            src_ref=src.at[target], dst_ref=dst.at[hd], send_sem=ssem.at[d], recv_sem=rsem.at[d],
            device_id={"head": target}, device_id_type=MESH,
        )

    def scene_gather(k, sending):
        sent, dev, arrives = (
            (p, nx, nx), (p, ny, ny), (p, nc, nc), (nx, ny, nd),
            (nx, nc, nx + flip), (ny, nc, ny + flip), (nd, nc, nd + flip),
        )[k]
        ref = scx.at[sent if sending else arrives]
        return copy(ref, ref, sx_send.at[k], sx_recv.at[k], dev)

    def scene_sum(k):
        src, dst, dev = (
            (nc, srsib.at[0], nc), (nx + flip, srsib.at[1], nc), (ny + flip, srsib.at[2], nc),
            (nd + flip, srsib.at[3], nc), (nd, srdiag, nx), (nx, srdir.at[0], nx),
            (ny, srdir.at[1], ny),
        )[k]
        return copy(scg.at[src], dst, sr_send.at[k], sr_recv.at[k], dev)

    def scene_row(h, half):
        return (half * heads + h) * n_head

    for d in range(1, n_head):
        scene(d, sc_src, sc_recv, sc_ssem, sc_rsem).start()
    for h in range(min(2, heads)):
        for k in range(3):
            ag(h, k, True).start()
    sc_recv[hd] = sc_src[hd]
    for h in range(2, heads):
        pack(h)
    for d in range(1, n_head):
        scene(d, sc_src, sc_recv, sc_ssem, sc_rsem).wait()
    for h in range(heads):
        for half in range(2):
            for t in range(n_head):
                row = half * 8 + h
                at = scene_row(h, half) + t
                scx[p, at:at + 1, :] = sc_recv[t, row:row + 1, :]
    for k in range(3):
        scene_gather(k, True).start()

    lane = lax.broadcasted_iota(jnp.int32, (1, rows), 1)
    lane_block = lax.div(lane, BLK)
    row_in = lax.broadcasted_iota(jnp.int32, (BLK, rows), 0)
    named = []
    for r in range(RAND):
        row = jnp.zeros((1, rows), jnp.int32)
        for b in range(blocks):
            row = jnp.where(lane_block == b, pattern_ref[p * blocks + b, r], row)
        named.append(row)
    query_block = lane_block + p * blocks

    def fill(c, carry):
        gap = query_block - c
        n = jnp.where((gap <= 1) & (gap >= -1), 1, 0)
        for row in named:
            n = n + jnp.where(row == c, 1, 0)
        level = jnp.full((1, rows), NEG, F32)
        for times, log in ((1, 0.0), (2, 1.0), (3, 1.584962500721156), (4, 2.0)):
            level = jnp.where(n == times, log, level)
        at = pl.multiple_of(c * BLK, BLK)
        bias[pl.ds(at, BLK), :] = jnp.where(
            row_in < valid_ref[c], jnp.broadcast_to(level, (BLK, rows)), NEG
        )
        return carry

    lax.fori_loop(0, 8 * blocks, fill, 0)
    scene_gather(0, False).wait_recv()
    scene_gather(1, False).wait_recv()
    for k in (3, 4, 5):
        scene_gather(k, True).start()
    extra_row = lax.broadcasted_iota(jnp.int32, (SCENE_ROWS, rows), 0)
    bias[base:, :] = jnp.where(extra_row < tokens, 0.0, NEG)
    for h in range(heads):
        for half in range(2):
            kv[h, half, base + tokens:, :] = jnp.zeros((SCENE_ROWS - tokens, DH), BF16)

    count = jnp.zeros((1, rows), jnp.int32)
    for b in range(blocks):
        count = jnp.where(lane_block == b, valid_ref[p * blocks + b], count)
    live_lane = lane - lane_block * BLK < count
    in_block = lax.broadcasted_iota(jnp.int32, (BLK, DH), 0)
    for b in range(blocks):
        keep = in_block < valid_ref[p * blocks + b]
        for h in range(heads):
            part = g_ref[b * BLK:(b + 1) * BLK, h * DH:(h + 1) * DH].astype(F32)
            glive[b * BLK:(b + 1) * BLK, h * DH:(h + 1) * DH] = jnp.where(
                keep, part, 0.0
            ).astype(BF16)

    for h in range(heads):
        qt[h] = q_ref[:, h * DH:(h + 1) * DH].T
        gt[h] = glive[:, h * DH:(h + 1) * DH].T
    scene_gather(3, False).wait_recv()
    scene_gather(6, True).start()
    for k in (2, 4, 5, 6):
        scene_gather(k, False).wait_recv()
    for h in range(heads):
        for half in range(2):
            for i in range(8):
                at = scene_row(h, half)
                sc_all[h, half, i * n_head:(i + 1) * n_head, :] = scx[i, at:at + n_head, :]
            kv[h, half, base:base + tokens, :] = sc_all[h, half].astype(BF16)

    scale = DH ** (-0.5)
    scale2 = scale * 1.4426950408889634
    pieces = [(i * rows, rows) for i in range(8)] + [(base, SCENE_ROWS)]

    def folded(x, op):
        return op(x.reshape(x.shape[0] // 8, 8, rows), axis=0)

    def attend(h):
        cols = pl.ds(pl.multiple_of(h * DH, DH), DH)
        q_t = qt[h]
        g_t = gt[h]
        top = jnp.full((8, rows), NEG, F32)
        for start, size in pieces:
            at = slice(start, start + size)
            key = kv[h, 0, at, :]
            s = jnp.dot(key, q_t, preferred_element_type=F32) * scale2 + bias[at, :]
            sbuf[at, :] = s
            kt[:, at] = key.T
            top = jnp.maximum(top, folded(s, jnp.max))
        top = jnp.max(top, axis=0, keepdims=True)
        z = jnp.zeros((8, rows), F32)
        delta = jnp.zeros((8, rows), F32)
        for start, size in pieces:
            at = slice(start, start + size)
            value = kv[h, 1, at, :]
            e = jnp.exp2(sbuf[at, :] - top)
            dp = jnp.dot(value, g_t, preferred_element_type=F32)
            sbuf[at, :] = e
            dbuf[at, :] = dp
            vt[:, at] = value.T
            z = z + folded(e, jnp.sum)
            delta = delta + folded(e * dp, jnp.sum)
        inv = 1.0 / jnp.sum(z, axis=0, keepdims=True)
        delta = jnp.sum(delta, axis=0, keepdims=True) * inv
        inv_scale = inv * scale
        q = q_ref[:, cols]
        g = glive[:, cols]
        for start, size in pieces:
            at = slice(start, start + size)
            e = sbuf[at, :]
            pbuf[at, :] = (e * inv).astype(BF16)
            dsbuf[at, :] = (e * inv_scale * (dbuf[at, :] - delta)).astype(BF16)
        for start in range(0, base, 2 * rows):
            at = slice(start, start + 2 * rows)
            grads[h, 0, at, :] = jnp.dot(
                dsbuf[at, :], q, preferred_element_type=F32
            ).astype(BF16)
            grads[h, 1, at, :] = jnp.dot(
                pbuf[at, :], g, preferred_element_type=F32
            ).astype(BF16)
        at = slice(base, base + tokens)
        sc_all[h, 0] = jnp.dot(dsbuf[at, :], q, preferred_element_type=F32)
        sc_all[h, 1] = jnp.dot(pbuf[at, :], g, preferred_element_type=F32)
        for k in range(4):
            rs(h, k).start()
        out = jnp.dot(vt[...], pbuf[...], preferred_element_type=F32)
        att_ref[:, cols] = jnp.where(live_lane, out, 0.0).T.astype(BF16)
        gq = jnp.dot(kt[...], dsbuf[...], preferred_element_type=F32)
        gq_ref[:, cols] = gq.T.astype(BF16)

    def part(h, half, q):
        return grads[h, half, pl.ds(pl.multiple_of(q * slot, 16), slot), :].astype(F32)

    def keep_part(h, half, q, x):
        grads[h, half, pl.ds(pl.multiple_of(q * slot, 16), slot), :] = x.astype(BF16)

    def step(t, carry):
        @pl.when(t < heads)
        def _():
            ag(t, 0, False).wait_recv()
            ag(t, 1, False).wait_recv()
            for k in (3, 4, 5, 6):
                ag(t, k, True).start()

        @pl.when(t + 2 < heads)
        def _():
            for k in range(3):
                ag(t + 2, k, True).start()

        @pl.when((t >= 1) & (t < heads + 1))
        def _():
            ag(t - 1, 3, False).wait_recv()
            ag(t - 1, 4, False).wait_recv()
            ag(t - 1, 7, True).start()

        @pl.when((t >= 3) & (t < heads + 3))
        def _():
            h = t - 3
            for k in range(4):
                rs(h, k).wait_recv()
            for half in range(2):
                keep_part(h, half, nd, part(h, half, nd) + rsib[h, 3, half].astype(F32))
            rs(h, 4).start()
            rs(h, 5).start()

        @pl.when((t >= 4) & (t < heads + 4))
        def _():
            h = t - 4
            rs(h, 4).wait_recv()
            rs(h, 5).wait_recv()
            for k, q, half_in in ((1, nx, 1), (2, ny, 0)):
                for half in range(2):
                    x = part(h, half, q) + rsib[h, k, half].astype(F32)
                    if half == half_in:
                        x = x + rdiag[h, half].astype(F32)
                    keep_part(h, half, q, x)
                rs(h, 5 + k).start()

        @pl.when((t >= 2) & (t < heads + 2))
        def _():
            h = t - 2
            for k in (2, 5, 6, 7):
                ag(h, k, False).wait_recv()
            attend(h)

        @pl.when(t >= 5)
        def _():
            h = t - 5
            rs(h, 6).wait_recv()
            rs(h, 7).wait_recv()
            cols = pl.ds(pl.multiple_of(h * DH, DH), DH)
            for half, ref in ((0, gk_ref), (1, gv_ref)):
                x = part(h, half, p) + rsib[h, 0, half].astype(F32)
                x = x + rdir[h, 0, half].astype(F32) + rdir[h, 1, half].astype(F32)
                ref[:, cols] = x.astype(BF16)

        @pl.when(t == heads + 1)
        def _():
            for h in range(heads):
                for half in range(2):
                    at = scene_row(h, half)
                    for i in range(8):
                        scg[i, at:at + n_head, :] = sc_all[
                            h, half, i * n_head:(i + 1) * n_head, :
                        ]
            for k in range(4):
                scene_sum(k).start()

        @pl.when(t == heads + 2)
        def _():
            for k in range(4):
                scene_sum(k).wait_recv()
            scg[nd] = scg[nd] + srsib[3]
            scene_sum(4).start()

        @pl.when(t == heads + 3)
        def _():
            scene_sum(4).wait_recv()
            scg[nx] = scg[nx] + srsib[1]
            scg[ny] = scg[ny] + srsib[2] + srdiag[...]
            scene_sum(5).start()
            scene_sum(6).start()

        return carry

    lax.fori_loop(0, heads + 5, step, 0)

    scene_sum(5).wait_recv()
    scene_sum(6).wait_recv()
    scg[p] = scg[p] + srsib[0] + srdir[0] + srdir[1]
    sc_send[...] = jnp.zeros_like(sc_send)
    for h in range(heads):
        for half in range(2):
            for t in range(n_head):
                row = half * 8 + h
                at = scene_row(h, half) + t
                sc_send[t, row:row + 1, :] = scg[p, at:at + 1, :]
    for d in range(1, n_head):
        scene(d, sc_send, sg_ref, sg_ssem, sg_rsem).start()
    sg_ref[hd] = sc_send[hd]
    for d in range(1, n_head):
        scene(d, sc_send, sg_ref, sg_ssem, sg_rsem).wait()

    def drain(h, carry):
        for k in range(8):
            ag(h, k, True).wait_send()
            rs(h, k).wait_send()
        return carry

    lax.fori_loop(0, heads, drain, 0)
    for k in range(7):
        scene_gather(k, True).wait_send()
        scene_sum(k).wait_send()


def finish_kernel(
    heads, n_head, a_ref, b_ref, c_ref, d_ref, sg_ref, ao, bo, co, do, sko, svo, sems
):
    pairs = ((a_ref, ao), (b_ref, bo), (c_ref, co), (d_ref, do))
    moves = [pltpu.make_async_copy(x, y, sems.at[i]) for i, (x, y) in enumerate(pairs)]
    for move in moves:
        move.start()
    for t in range(n_head):
        for h in range(heads):
            at = (t * heads + h) * DH
            sko[:, at:at + DH] = sg_ref[t, h:h + 1, :].astype(BF16)
            svo[:, at:at + DH] = sg_ref[t, 8 + h:9 + h, :].astype(BF16)
    for move in moves:
        move.wait()


def fused_device(queries, keys, values, grad_out, scene_keys, scene_values, valid, pattern):
    n_head = lax.axis_size("head")
    rows, features = queries.shape
    heads = features // DH
    blocks = rows // BLK
    slot = rows
    base = 8 * slot
    total = base + SCENE_ROWS
    tokens = 8 * n_head
    flat = 2 * heads * n_head
    vmem = pl.BlockSpec(memory_space=pltpu.VMEM)
    anywhere = pl.BlockSpec(memory_space=pl.ANY)
    smem = pl.BlockSpec(memory_space=pltpu.SMEM)
    wide = jax.ShapeDtypeStruct((rows, features), BF16)
    dma = pltpu.SemaphoreType.DMA
    out = pl.pallas_call(
        functools.partial(fused_kernel, heads, n_head, blocks),
        out_shape=[wide] * 4 + [jax.ShapeDtypeStruct((n_head, 16, DH), F32)],
        in_specs=[smem, smem] + [vmem] * 6,
        out_specs=[vmem] * 5,
        scratch_shapes=[
            pltpu.VMEM((heads, 2, total, DH), BF16),
            pltpu.VMEM((heads, 2, base, DH), BF16),
            pltpu.VMEM((heads, 4, 2, slot, DH), BF16),
            pltpu.VMEM((heads, 2, slot, DH), BF16),
            pltpu.VMEM((heads, 2, 2, slot, DH), BF16),
            pltpu.VMEM((total, rows), F32),
            pltpu.VMEM((total, rows), F32),
            pltpu.VMEM((total, rows), F32),
            pltpu.VMEM((total, rows), BF16),
            pltpu.VMEM((total, rows), BF16),
            pltpu.VMEM((DH, total), BF16),
            pltpu.VMEM((DH, total), BF16),
            pltpu.VMEM((rows, features), BF16),
            pltpu.VMEM((heads, DH, rows), BF16),
            pltpu.VMEM((heads, DH, rows), BF16),
            pltpu.VMEM((n_head, 16, DH), F32),
            pltpu.VMEM((n_head, 16, DH), F32),
            pltpu.VMEM((n_head, 16, DH), F32),
            pltpu.VMEM((8, flat, DH), F32),
            pltpu.VMEM((heads, 2, tokens, DH), F32),
            pltpu.VMEM((8, flat, DH), F32),
            pltpu.VMEM((4, flat, DH), F32),
            pltpu.VMEM((flat, DH), F32),
            pltpu.VMEM((2, flat, DH), F32),
            dma((heads, 8)), dma((heads, 8)), dma((heads, 8)), dma((heads, 8)),
            dma((n_head,)), dma((n_head,)), dma((n_head,)), dma((n_head,)),
            dma((7,)), dma((7,)), dma((7,)), dma((7,)),
        ],
        compiler_params=pltpu.CompilerParams(
            collective_id=0, has_side_effects=True, vmem_limit_bytes=52 * 1024 * 1024
        ),
    )(valid, pattern, queries, keys, values, grad_out, scene_keys, scene_values)
    row = jax.ShapeDtypeStruct((1, n_head * features), BF16)
    return tuple(
        pl.pallas_call(
            functools.partial(finish_kernel, heads, n_head),
            out_shape=[wide] * 4 + [row] * 2,
            in_specs=[anywhere] * 4 + [vmem],
            out_specs=[anywhere] * 4 + [vmem] * 2,
            scratch_shapes=[dma((4,))],
        )(*out)
    )


def solution(mesh):
    placed = (
        P("seq", "head"),
        P("seq", "head"),
        P("seq", "head"),
        P("seq", "head"),
        P(("seq", "head"), None),
        P(("seq", "head"), None),
        P(),
        P(),
    )
    body = fused_device if mesh.shape["seq"] == 8 else per_device
    return jax.shard_map(
        body,
        mesh=mesh,
        in_specs=placed,
        out_specs=(
            P("seq", "head"),
            P("seq", "head"),
            P("seq", "head"),
            P("seq", "head"),
            P(("seq", "head"), None),
            P(("seq", "head"), None),
        ),
        check_vma=False,
    )
```

```python
import functools

import jax
import jax.numpy as jnp
from jax import lax
from jax.experimental import pallas as pl
from jax.experimental.pallas import tpu as pltpu
from jax.sharding import PartitionSpec as P

DH = 128
BLK = 64
RAND = 3


def extended_2(block, sides, width):
    for axis, dim in sides:
        count = lax.axis_size(axis)
        forward = [(i, i + 1) for i in range(count - 1)]
        backward = [(target, source) for source, target in forward]
        low = lax.ppermute(
            lax.slice_in_dim(block, block.shape[dim] - width, None, axis=dim), axis, forward
        )
        high = lax.ppermute(lax.slice_in_dim(block, 0, width, axis=dim), axis, backward)
        block = jnp.concatenate([low, block, high], axis=dim)
    return block


def passed_along(x, axis, by):
    length = lax.axis_size(axis)
    pairs = [(i, i + by) for i in range(length) if 0 <= i + by < length]
    return lax.ppermute(x, axis, pairs)


def block_terms(query, all_keys, all_values, key_live, query_live, grad_out):
    scale = DH ** (-0.5)
    scores = (
        jnp.einsum("gqhd,gkhd->ghqk", query, all_keys, preferred_element_type=jnp.float32) * scale
    )
    scores = jnp.where(key_live[:, None, None, :], scores, -1e30)
    highest = jnp.max(scores, axis=3, keepdims=True)
    expo = jnp.exp(scores - highest)
    prob = expo / jnp.sum(expo, axis=3, keepdims=True)
    prob_round = prob.astype(jnp.bfloat16)
    live_rows = query_live[:, :, None, None]
    attended = jnp.einsum(
        "ghqk,gkhd->gqhd", prob_round, all_values, preferred_element_type=jnp.float32
    )
    attended = jnp.where(live_rows, attended, 0.0).astype(jnp.bfloat16)
    grad_live = jnp.where(live_rows, grad_out, 0.0)
    dprob = jnp.einsum("gqhd,gkhd->ghqk", grad_live, all_values, preferred_element_type=jnp.float32)
    delta = jnp.sum(prob * dprob, axis=3, keepdims=True)
    dscore = (prob * (dprob - delta) * scale).astype(jnp.bfloat16)
    grad_query = jnp.einsum("ghqk,gkhd->gqhd", dscore, all_keys, preferred_element_type=jnp.float32)
    grad_k = jnp.einsum("ghqk,gqhd->gkhd", dscore, query, preferred_element_type=jnp.float32)
    grad_v = jnp.einsum(
        "ghqk,gqhd->gkhd", prob_round, grad_live, preferred_element_type=jnp.float32
    )
    return (attended, grad_query.astype(jnp.bfloat16), grad_k, grad_v)


def per_device(queries, keys, values, grad_out, scene_keys, scene_values, valid, pattern):
    seq_count = lax.axis_size("seq")
    position = lax.axis_index("seq")
    features = queries.shape[1]
    head_count = features // DH
    blocks_dev = queries.shape[0] // BLK
    group_size = min(8, blocks_dev)
    requests = blocks_dev * RAND
    slot_count = (requests + seq_count - 2) // (seq_count - 1)
    offsets = jnp.arange(BLK, dtype=jnp.int32)
    near_count = (3 + RAND) * BLK
    parted = (
        lax.all_to_all(scene_keys, "head", split_axis=1, concat_axis=0, tiled=True),
        lax.all_to_all(scene_values, "head", split_axis=1, concat_axis=0, tiled=True),
    )
    scene_k, scene_v = (
        lax.all_gather(parted[0], "seq", axis=0, tiled=True),
        lax.all_gather(parted[1], "seq", axis=0, tiled=True),
    )
    scene_rows_all = scene_k.shape[0]
    scene_kv = jnp.stack([scene_k, scene_v]).reshape(2, 1, scene_rows_all, head_count, DH)
    scene_kv = jnp.broadcast_to(scene_kv, (2, group_size, scene_rows_all, head_count, DH))
    stacked = jnp.stack([keys, values])
    extended = extended_2(stacked, (("seq", 1),), BLK)
    all_requests = pattern.reshape(seq_count, requests)
    source = all_requests // blocks_dev
    local_block = all_requests % blocks_dev
    from_here = source == position
    send_rank = jnp.cumsum(from_here.astype(jnp.int32), axis=1) - 1
    slot_ids = jnp.arange(slot_count, dtype=jnp.int32)
    marked = from_here[:, :, None] & (send_rank[:, :, None] == slot_ids[None, None, :])
    chosen = jnp.sum(jnp.where(marked, local_block[:, :, None], 0), axis=1)
    block_view = stacked.reshape(2, blocks_dev, BLK, features)
    outgoing = block_view[:, chosen]
    incoming = lax.all_to_all(outgoing, "seq", split_axis=1, concat_axis=1, tiled=True)
    own_requests = lax.dynamic_slice_in_dim(pattern, position * blocks_dev, blocks_dev, 0).reshape(
        requests
    )
    own_source = own_requests // blocks_dev
    earlier = jnp.tril(jnp.ones((requests, requests), jnp.bool_), -1)
    same_source = own_source[:, None] == own_source[None, :]
    recv_rank = jnp.sum((same_source & earlier).astype(jnp.int32), axis=1)
    recv_place = own_source * slot_count + recv_rank
    far_blocks = incoming.reshape(2, seq_count * slot_count, BLK, features)[:, recv_place]
    far_blocks = far_blocks.reshape(2, blocks_dev, RAND, BLK, features)
    padded_valid = jnp.concatenate([jnp.zeros((1,), jnp.int32), valid, jnp.zeros((1,), jnp.int32)])
    window_count = lax.dynamic_slice_in_dim(padded_valid, position * blocks_dev, blocks_dev + 2, 0)
    far_count = valid[own_requests].reshape(blocks_dev, RAND)
    query_count = lax.dynamic_slice_in_dim(valid, position * blocks_dev, blocks_dev, 0)
    scene_live = jnp.ones((group_size, scene_rows_all), jnp.bool_)
    ext_grad = jnp.zeros((2, blocks_dev + 2, BLK, features), jnp.float32)
    query_grp = queries.reshape(group_size, BLK, head_count, DH)
    grad_grp = grad_out.reshape(group_size, BLK, head_count, DH)
    window = extended.reshape(2, group_size + 2, BLK, features)
    near_kv = jnp.concatenate(
        [
            window[:, 0:group_size, None],
            window[:, 1 : group_size + 1, None],
            window[:, 2:, None],
            far_blocks,
        ],
        axis=2,
    )
    near_kv = near_kv.reshape(2, group_size, near_count, head_count, DH)
    joined_kv = jnp.concatenate([near_kv, scene_kv], axis=2)
    counts = jnp.concatenate(
        [
            window_count[0:group_size, None],
            window_count[1 : group_size + 1, None],
            window_count[2 : group_size + 2, None],
            far_count,
        ],
        axis=1,
    )
    near_live = (offsets[None, None, :] < counts[:, :, None]).reshape(group_size, near_count)
    key_live = jnp.concatenate([near_live, scene_live], axis=1)
    query_live = offsets[None, :] < query_count[0:group_size, None]
    attended, grad_query, grad_k, grad_v = block_terms(
        query_grp, joined_kv[0], joined_kv[1], key_live, query_live, grad_grp
    )
    both_grad = jnp.stack([grad_k, grad_v])
    near_grad = both_grad[:, :, :near_count].reshape(2, group_size, 3 + RAND, BLK, features)
    scene_grad = jnp.sum(both_grad[:, :, near_count:], axis=1)
    ext_grad = ext_grad.at[:, 0:group_size].add(near_grad[:, :, 0])
    ext_grad = ext_grad.at[:, 1 : group_size + 1].add(near_grad[:, :, 1])
    ext_grad = ext_grad.at[:, 2 : group_size + 2].add(near_grad[:, :, 2])
    random_parts = near_grad[:, :, 3:].astype(jnp.bfloat16)
    attended_parts = attended.reshape(group_size * BLK, features)
    query_parts = grad_query.reshape(group_size * BLK, features)
    random_terms = random_parts.reshape(2, requests, BLK, features)
    outgoing_grad = (
        jnp.zeros((2, seq_count * slot_count, BLK, features), jnp.bfloat16)
        .at[:, recv_place]
        .set(random_terms)
    )
    outgoing_grad = outgoing_grad.reshape(2, seq_count, slot_count, BLK, features)
    returned = lax.all_to_all(outgoing_grad, "seq", split_axis=1, concat_axis=1, tiled=True)
    selector = (
        chosen.reshape(-1)[:, None] == jnp.arange(blocks_dev, dtype=jnp.int32)[None, :]
    ).astype(jnp.bfloat16)
    gathered_grad = jnp.einsum(
        "sb,xsk->xbk",
        selector,
        returned.reshape(2, seq_count * slot_count, BLK * features),
        preferred_element_type=jnp.float32,
    )
    from_right = passed_along(ext_grad[:, 0].astype(jnp.bfloat16), "seq", -1).astype(jnp.float32)
    from_left = passed_along(ext_grad[:, blocks_dev + 1].astype(jnp.bfloat16), "seq", 1).astype(
        jnp.float32
    )
    inner = ext_grad[:, 1 : blocks_dev + 1]
    inner = inner.at[:, blocks_dev - 1].add(from_right).at[:, 0].add(from_left)
    total_grad = inner.reshape(2, blocks_dev, BLK * features) + gathered_grad
    grad_keys = total_grad[0].reshape(blocks_dev * BLK, features).astype(jnp.bfloat16)
    grad_values = total_grad[1].reshape(blocks_dev * BLK, features).astype(jnp.bfloat16)
    scene_terms_k = scene_grad[0].reshape(scene_rows_all, features)
    scene_terms_v = scene_grad[1].reshape(scene_rows_all, features)
    mine_k, mine_v = (
        lax.psum_scatter(scene_terms_k, "seq", scatter_dimension=0, tiled=True),
        lax.psum_scatter(scene_terms_v, "seq", scatter_dimension=0, tiled=True),
    )
    back_k, back_v = (
        lax.all_to_all(mine_k, "head", split_axis=0, concat_axis=1, tiled=True),
        lax.all_to_all(mine_v, "head", split_axis=0, concat_axis=1, tiled=True),
    )
    return (
        attended_parts,
        query_parts,
        grad_keys,
        grad_values,
        back_k.astype(jnp.bfloat16),
        back_v.astype(jnp.bfloat16),
    )


NEG = -1e30
SCENE_ROWS = 128
MESH = pl.DeviceIdType.MESH
F32 = jnp.float32
BF16 = jnp.bfloat16


def fused_kernel(
    heads, n_head, blocks,
    valid_ref, pattern_ref, q_ref, k_ref, v_ref, g_ref, sk_ref, sv_ref,
    att_ref, gq_ref, gk_ref, gv_ref, sg_ref,
    kv, grads, rsib, rdiag, rdir, bias, sbuf, dbuf, pbuf, dsbuf, kt, vt, glive, qt, gt,
    sc_src, sc_recv, sc_send, scx, sc_all, scg, srsib, srdiag, srdir,
    ag_send, ag_recv, rs_send, rs_recv, sc_ssem, sc_rsem, sg_ssem, sg_rsem,
    sx_send, sx_recv, sr_send, sr_recv,
):
    rows = blocks * BLK
    slot = rows
    base = 8 * slot
    total = base + SCENE_ROWS
    tokens = 8 * n_head
    p = lax.axis_index("seq")
    hd = lax.axis_index("head")
    nc = p + 1 - 2 * lax.rem(p, 2)
    nx = p + 2 - 4 * lax.rem(lax.div(p, 2), 2)
    ny = p + 4 - 8 * lax.rem(lax.div(p, 4), 2)
    nd = nx + ny - p
    flip = nc - p
    own = pl.multiple_of(p * slot, 16)

    def pack(h):
        kv[h, 0, pl.ds(own, rows), :] = k_ref[:, h * DH:(h + 1) * DH]
        kv[h, 1, pl.ds(own, rows), :] = v_ref[:, h * DH:(h + 1) * DH]

    barrier = pltpu.get_barrier_semaphore()
    for target in (nc, nx, ny):
        pl.semaphore_signal(barrier, inc=1, device_id={"seq": target}, device_id_type=MESH)
    for d in range(1, n_head):
        pl.semaphore_signal(
            barrier, inc=1, device_id={"head": lax.rem(hd + d, n_head)}, device_id_type=MESH
        )
    for h in range(min(2, heads)):
        pack(h)
    sc_src[...] = jnp.zeros_like(sc_src)
    for t in range(n_head):
        for h in range(heads):
            at = (t * heads + h) * DH
            sc_src[t, h:h + 1, :] = sk_ref[:, at:at + DH].astype(F32)
            sc_src[t, 8 + h:9 + h, :] = sv_ref[:, at:at + DH].astype(F32)
    pl.semaphore_wait(barrier, 3 + n_head - 1)

    def at_slot(ref, h, q):
        return ref.at[h, :, pl.ds(pl.multiple_of(q * slot, 16), slot), :]

    def at_half(ref, h, half, q):
        return ref.at[h, half, pl.ds(pl.multiple_of(q * slot, 16), slot), :]

    def copy(src, dst, ssem, rsem, dev):
        return pltpu.make_async_remote_copy(
            src_ref=src, dst_ref=dst, send_sem=ssem, recv_sem=rsem,
            device_id={"seq": dev}, device_id_type=MESH,
        )

    def ag(h, k, sending):
        sent, dev, arrives = (
            (p, nx, nx), (p, ny, ny), (p, nc, nc), (nx, ny, nd), (ny, nx, nd),
            (nx, nc, nx + flip), (ny, nc, ny + flip), (nd, nc, nd + flip),
        )[k]
        s = sent if sending else arrives
        ref = at_half(kv, h, k - 3, s) if k in (3, 4) else at_slot(kv, h, s)
        return copy(ref, ref, ag_send.at[h, k], ag_recv.at[h, k], dev)

    def rs(h, k):
        if k < 4:
            q = (p, nx, ny, nd)[k] + flip
            src, dst, dev = at_slot(grads, h, q), rsib.at[h, k], nc
        elif k < 6:
            src, dst = at_half(grads, h, k - 4, nd), rdiag.at[h, k - 4]
            dev = (nx, ny)[k - 4]
        else:
            dev = (nx, ny)[k - 6]
            src, dst = at_slot(grads, h, dev), rdir.at[h, k - 6]
        return copy(src, dst, rs_send.at[h, k], rs_recv.at[h, k], dev)

    def scene(d, src, dst, ssem, rsem):
        target = lax.rem(hd + d, n_head)
        return pltpu.make_async_remote_copy(
            src_ref=src.at[target], dst_ref=dst.at[hd], send_sem=ssem.at[d], recv_sem=rsem.at[d],
            device_id={"head": target}, device_id_type=MESH,
        )

    def scene_gather(k, sending):
        sent, dev, arrives = (
            (p, nx, nx), (p, ny, ny), (p, nc, nc), (nx, ny, nd),
            (nx, nc, nx + flip), (ny, nc, ny + flip), (nd, nc, nd + flip),
        )[k]
        ref = scx.at[sent if sending else arrives]
        return copy(ref, ref, sx_send.at[k], sx_recv.at[k], dev)

    def scene_sum(k):
        src, dst, dev = (
            (nc, srsib.at[0], nc), (nx + flip, srsib.at[1], nc), (ny + flip, srsib.at[2], nc),
            (nd + flip, srsib.at[3], nc), (nd, srdiag, nx), (nx, srdir.at[0], nx),
            (ny, srdir.at[1], ny),
        )[k]
        return copy(scg.at[src], dst, sr_send.at[k], sr_recv.at[k], dev)

    def scene_row(h, half):
        return (half * heads + h) * n_head

    for d in range(1, n_head):
        scene(d, sc_src, sc_recv, sc_ssem, sc_rsem).start()
    for h in range(min(2, heads)):
        for k in range(3):
            ag(h, k, True).start()
    sc_recv[hd] = sc_src[hd]
    for h in range(2, heads):
        pack(h)
    for d in range(1, n_head):
        scene(d, sc_src, sc_recv, sc_ssem, sc_rsem).wait()
    for h in range(heads):
        for half in range(2):
            for t in range(n_head):
                row = half * 8 + h
                at = scene_row(h, half) + t
                scx[p, at:at + 1, :] = sc_recv[t, row:row + 1, :]
    for k in range(3):
        scene_gather(k, True).start()

    lane = lax.broadcasted_iota(jnp.int32, (1, rows), 1)
    lane_block = lax.div(lane, BLK)
    row_in = lax.broadcasted_iota(jnp.int32, (BLK, rows), 0)
    named = []
    for r in range(RAND):
        row = jnp.zeros((1, rows), jnp.int32)
        for b in range(blocks):
            row = jnp.where(lane_block == b, pattern_ref[p * blocks + b, r], row)
        named.append(row)
    query_block = lane_block + p * blocks

    def fill(c, carry):
        gap = query_block - c
        n = jnp.where((gap <= 1) & (gap >= -1), 1, 0)
        for row in named:
            n = n + jnp.where(row == c, 1, 0)
        level = jnp.full((1, rows), NEG, F32)
        for times, log in ((1, 0.0), (2, 1.0), (3, 1.584962500721156), (4, 2.0)):
            level = jnp.where(n == times, log, level)
        at = pl.multiple_of(c * BLK, BLK)
        bias[pl.ds(at, BLK), :] = jnp.where(
            row_in < valid_ref[c], jnp.broadcast_to(level, (BLK, rows)), NEG
        )
        return carry

    lax.fori_loop(0, 8 * blocks, fill, 0)
    scene_gather(0, False).wait_recv()
    scene_gather(1, False).wait_recv()
    for k in (3, 4, 5):
        scene_gather(k, True).start()
    extra_row = lax.broadcasted_iota(jnp.int32, (SCENE_ROWS, rows), 0)
    bias[base:, :] = jnp.where(extra_row < tokens, 0.0, NEG)
    for h in range(heads):
        for half in range(2):
            kv[h, half, base + tokens:, :] = jnp.zeros((SCENE_ROWS - tokens, DH), BF16)

    count = jnp.zeros((1, rows), jnp.int32)
    for b in range(blocks):
        count = jnp.where(lane_block == b, valid_ref[p * blocks + b], count)
    live_lane = lane - lane_block * BLK < count
    in_block = lax.broadcasted_iota(jnp.int32, (BLK, DH), 0)
    for b in range(blocks):
        keep = in_block < valid_ref[p * blocks + b]
        for h in range(heads):
            part = g_ref[b * BLK:(b + 1) * BLK, h * DH:(h + 1) * DH].astype(F32)
            glive[b * BLK:(b + 1) * BLK, h * DH:(h + 1) * DH] = jnp.where(
                keep, part, 0.0
            ).astype(BF16)

    for h in range(heads):
        qt[h] = q_ref[:, h * DH:(h + 1) * DH].T
        gt[h] = glive[:, h * DH:(h + 1) * DH].T
    scene_gather(3, False).wait_recv()
    scene_gather(6, True).start()
    for k in (2, 4, 5, 6):
        scene_gather(k, False).wait_recv()
    for h in range(heads):
        for half in range(2):
            for i in range(8):
                at = scene_row(h, half)
                sc_all[h, half, i * n_head:(i + 1) * n_head, :] = scx[i, at:at + n_head, :]
            kv[h, half, base:base + tokens, :] = sc_all[h, half].astype(BF16)

    scale = DH ** (-0.5)
    scale2 = scale * 1.4426950408889634
    pieces = [(i * rows, rows) for i in range(8)] + [(base, SCENE_ROWS)]

    def folded(x, op):
        return op(x.reshape(x.shape[0] // 8, 8, rows), axis=0)

    def attend(h):
        cols = pl.ds(pl.multiple_of(h * DH, DH), DH)
        q_t = qt[h]
        g_t = gt[h]
        top = jnp.full((8, rows), NEG, F32)
        for start, size in pieces:
            at = slice(start, start + size)
            key = kv[h, 0, at, :]
            s = jnp.dot(key, q_t, preferred_element_type=F32) * scale2 + bias[at, :]
            sbuf[at, :] = s
            kt[:, at] = key.T
            top = jnp.maximum(top, folded(s, jnp.max))
        top = jnp.max(top, axis=0, keepdims=True)
        z = jnp.zeros((8, rows), F32)
        delta = jnp.zeros((8, rows), F32)
        for start, size in pieces:
            at = slice(start, start + size)
            value = kv[h, 1, at, :]
            e = jnp.exp2(sbuf[at, :] - top)
            dp = jnp.dot(value, g_t, preferred_element_type=F32)
            sbuf[at, :] = e
            dbuf[at, :] = dp
            vt[:, at] = value.T
            z = z + folded(e, jnp.sum)
            delta = delta + folded(e * dp, jnp.sum)
        inv = 1.0 / jnp.sum(z, axis=0, keepdims=True)
        delta = jnp.sum(delta, axis=0, keepdims=True) * inv
        inv_scale = inv * scale
        q = q_ref[:, cols]
        g = glive[:, cols]
        for start, size in pieces:
            at = slice(start, start + size)
            e = sbuf[at, :]
            pbuf[at, :] = (e * inv).astype(BF16)
            dsbuf[at, :] = (e * inv_scale * (dbuf[at, :] - delta)).astype(BF16)
        for start in range(0, base, 2 * rows):
            at = slice(start, start + 2 * rows)
            grads[h, 0, at, :] = jnp.dot(
                dsbuf[at, :], q, preferred_element_type=F32
            ).astype(BF16)
            grads[h, 1, at, :] = jnp.dot(
                pbuf[at, :], g, preferred_element_type=F32
            ).astype(BF16)
        at = slice(base, base + tokens)
        sc_all[h, 0] = jnp.dot(dsbuf[at, :], q, preferred_element_type=F32)
        sc_all[h, 1] = jnp.dot(pbuf[at, :], g, preferred_element_type=F32)
        for k in range(4):
            rs(h, k).start()
        out = jnp.dot(vt[...], pbuf[...], preferred_element_type=F32)
        att_ref[:, cols] = jnp.where(live_lane, out, 0.0).T.astype(BF16)
        gq = jnp.dot(kt[...], dsbuf[...], preferred_element_type=F32)
        gq_ref[:, cols] = gq.T.astype(BF16)

    def part(h, half, q):
        return grads[h, half, pl.ds(pl.multiple_of(q * slot, 16), slot), :].astype(F32)

    def keep_part(h, half, q, x):
        grads[h, half, pl.ds(pl.multiple_of(q * slot, 16), slot), :] = x.astype(BF16)

    def step(t, carry):
        @pl.when(t < heads)
        def _():
            ag(t, 0, False).wait_recv()
            ag(t, 1, False).wait_recv()
            for k in (3, 4, 5, 6):
                ag(t, k, True).start()

        @pl.when(t + 2 < heads)
        def _():
            for k in range(3):
                ag(t + 2, k, True).start()

        @pl.when((t >= 1) & (t < heads + 1))
        def _():
            ag(t - 1, 3, False).wait_recv()
            ag(t - 1, 4, False).wait_recv()
            ag(t - 1, 7, True).start()

        @pl.when((t >= 3) & (t < heads + 3))
        def _():
            h = t - 3
            for k in range(4):
                rs(h, k).wait_recv()
            for half in range(2):
                keep_part(h, half, nd, part(h, half, nd) + rsib[h, 3, half].astype(F32))
            rs(h, 4).start()
            rs(h, 5).start()

        @pl.when((t >= 4) & (t < heads + 4))
        def _():
            h = t - 4
            rs(h, 4).wait_recv()
            rs(h, 5).wait_recv()
            for k, q, half_in in ((1, nx, 1), (2, ny, 0)):
                for half in range(2):
                    x = part(h, half, q) + rsib[h, k, half].astype(F32)
                    if half == half_in:
                        x = x + rdiag[h, half].astype(F32)
                    keep_part(h, half, q, x)
                rs(h, 5 + k).start()

        @pl.when((t >= 2) & (t < heads + 2))
        def _():
            h = t - 2
            for k in (2, 5, 6, 7):
                ag(h, k, False).wait_recv()
            attend(h)

        @pl.when(t >= 5)
        def _():
            h = t - 5
            rs(h, 6).wait_recv()
            rs(h, 7).wait_recv()
            cols = pl.ds(pl.multiple_of(h * DH, DH), DH)
            for half, ref in ((0, gk_ref), (1, gv_ref)):
                x = part(h, half, p) + rsib[h, 0, half].astype(F32)
                x = x + rdir[h, 0, half].astype(F32) + rdir[h, 1, half].astype(F32)
                ref[:, cols] = x.astype(BF16)

        @pl.when(t == heads + 1)
        def _():
            for h in range(heads):
                for half in range(2):
                    at = scene_row(h, half)
                    for i in range(8):
                        scg[i, at:at + n_head, :] = sc_all[
                            h, half, i * n_head:(i + 1) * n_head, :
                        ]
            for k in range(4):
                scene_sum(k).start()

        @pl.when(t == heads + 2)
        def _():
            for k in range(4):
                scene_sum(k).wait_recv()
            scg[nd] = scg[nd] + srsib[3]
            scene_sum(4).start()

        @pl.when(t == heads + 3)
        def _():
            scene_sum(4).wait_recv()
            scg[nx] = scg[nx] + srsib[1]
            scg[ny] = scg[ny] + srsib[2] + srdiag[...]
            scene_sum(5).start()
            scene_sum(6).start()

        return carry

    lax.fori_loop(0, heads + 5, step, 0)

    scene_sum(5).wait_recv()
    scene_sum(6).wait_recv()
    scg[p] = scg[p] + srsib[0] + srdir[0] + srdir[1]
    sc_send[...] = jnp.zeros_like(sc_send)
    for h in range(heads):
        for half in range(2):
            for t in range(n_head):
                row = half * 8 + h
                at = scene_row(h, half) + t
                sc_send[t, row:row + 1, :] = scg[p, at:at + 1, :]
    for d in range(1, n_head):
        scene(d, sc_send, sg_ref, sg_ssem, sg_rsem).start()
    sg_ref[hd] = sc_send[hd]
    for d in range(1, n_head):
        scene(d, sc_send, sg_ref, sg_ssem, sg_rsem).wait()

    def drain(h, carry):
        for k in range(8):
            ag(h, k, True).wait_send()
            rs(h, k).wait_send()
        return carry

    lax.fori_loop(0, heads, drain, 0)
    for k in range(7):
        scene_gather(k, True).wait_send()
        scene_sum(k).wait_send()


def fused_device(queries, keys, values, grad_out, scene_keys, scene_values, valid, pattern):
    n_head = lax.axis_size("head")
    rows, features = queries.shape
    heads = features // DH
    blocks = rows // BLK
    slot = rows
    base = 8 * slot
    total = base + SCENE_ROWS
    tokens = 8 * n_head
    flat = 2 * heads * n_head
    vmem = pl.BlockSpec(memory_space=pltpu.VMEM)
    smem = pl.BlockSpec(memory_space=pltpu.SMEM)
    wide = jax.ShapeDtypeStruct((rows, features), BF16)
    dma = pltpu.SemaphoreType.DMA
    out = pl.pallas_call(
        functools.partial(fused_kernel, heads, n_head, blocks),
        out_shape=[wide] * 4 + [jax.ShapeDtypeStruct((n_head, 16, DH), F32)],
        in_specs=[smem, smem] + [vmem] * 6,
        out_specs=[vmem] * 5,
        scratch_shapes=[
            pltpu.VMEM((heads, 2, total, DH), BF16),
            pltpu.VMEM((heads, 2, base, DH), BF16),
            pltpu.VMEM((heads, 4, 2, slot, DH), BF16),
            pltpu.VMEM((heads, 2, slot, DH), BF16),
            pltpu.VMEM((heads, 2, 2, slot, DH), BF16),
            pltpu.VMEM((total, rows), F32),
            pltpu.VMEM((total, rows), F32),
            pltpu.VMEM((total, rows), F32),
            pltpu.VMEM((total, rows), BF16),
            pltpu.VMEM((total, rows), BF16),
            pltpu.VMEM((DH, total), BF16),
            pltpu.VMEM((DH, total), BF16),
            pltpu.VMEM((rows, features), BF16),
            pltpu.VMEM((heads, DH, rows), BF16),
            pltpu.VMEM((heads, DH, rows), BF16),
            pltpu.VMEM((n_head, 16, DH), F32),
            pltpu.VMEM((n_head, 16, DH), F32),
            pltpu.VMEM((n_head, 16, DH), F32),
            pltpu.VMEM((8, flat, DH), F32),
            pltpu.VMEM((heads, 2, tokens, DH), F32),
            pltpu.VMEM((8, flat, DH), F32),
            pltpu.VMEM((4, flat, DH), F32),
            pltpu.VMEM((flat, DH), F32),
            pltpu.VMEM((2, flat, DH), F32),
            dma((heads, 8)), dma((heads, 8)), dma((heads, 8)), dma((heads, 8)),
            dma((n_head,)), dma((n_head,)), dma((n_head,)), dma((n_head,)),
            dma((7,)), dma((7,)), dma((7,)), dma((7,)),
        ],
        compiler_params=pltpu.CompilerParams(
            collective_id=0, has_side_effects=True, vmem_limit_bytes=52 * 1024 * 1024
        ),
    )(valid, pattern, queries, keys, values, grad_out, scene_keys, scene_values)
    att, gq, gk, gv, sg = out
    gsk = sg[:, :heads].reshape(1, n_head * features).astype(BF16)
    gsv = sg[:, 8:8 + heads].reshape(1, n_head * features).astype(BF16)
    return att, gq, gk, gv, gsk, gsv


def solution(mesh):
    placed = (
        P("seq", "head"),
        P("seq", "head"),
        P("seq", "head"),
        P("seq", "head"),
        P(("seq", "head"), None),
        P(("seq", "head"), None),
        P(),
        P(),
    )
    body = fused_device if mesh.shape["seq"] == 8 else per_device
    return jax.shard_map(
        body,
        mesh=mesh,
        in_specs=placed,
        out_specs=(
            P("seq", "head"),
            P("seq", "head"),
            P("seq", "head"),
            P("seq", "head"),
            P(("seq", "head"), None),
            P(("seq", "head"), None),
        ),
        check_vma=False,
    )
```
